32 devices in a mesh: gx: 8 (over z, x), gy: 4 (over y, core).
Axes of the slice: x: 2, y: 2, z: 4, core: 2. Of those that a mesh axis runs over, the one named last changes fastest.
Arguments:
- rhs_field: float32 [2, 8, 64, 1024], P(None, None, 'gx', 'gy'), may hold values from -6 to 6
- permittivity: float32 [8, 64, 1024], P(None, 'gx', 'gy'), may hold values from 1 to 4
- surf_dist: float32 [1024, 128], P(('gx', 'gy')), may hold values from 0.2 to 1
- surf_normal: float32 [3, 1024, 128], P(None, ('gx', 'gy')), may hold values from -4 to 4
- surf_inc: float32 [2, 1024, 128], P(None, ('gx', 'gy')), may hold values from -6 to 6
- surf_cell: int32 [1024, 128], P(('gx', 'gy')), may hold values from 0 to 16383
- surf_mask: int32 [1024, 128], P(('gx', 'gy')), may hold values 0 or 1
- surf_owner: int32 [1024, 1], P(('gx', 'gy')), may hold values from 0 to 31; in each aligned block of 32 rows (0 to 31, 32 to 63, ...) at most 2 rows name the same one
Outputs:
- solution: float32 [2, 8, 64, 1024], P(None, None, 'gx', 'gy')
- residual: float32 [2, 8, 64, 1024], P(None, None, 'gx', 'gy')
The draws below stay inside these ranges and needn't reach their ends.
Inputs may be any that keep to these rules, and one draw needn't show every extreme that they name: `surf_owner`: within the 32 rows of one device no owner is named more than 2 times, a bound that some block reaches.
All inputs are finite; a program needn't handle non-finite values. No bound on the sum of `surf_mask` on one device may be relied on, other than what follows from the above.
Results may differ from the reference program's by a relative error of at most 0.00002.
Values sent between devices are 32-bit elements; how exact they have to be, the bound alone decides.
A program may use at most 128 MiB of HBM per device.

```python
import math
import jax
import jax.numpy as jnp
import numpy as np

NZ = 8
CX = 8
CY = 256
PTS = 128
CAP = 2
ITERS = 2
SWEEPS = 2
SB = 32
NB = 1024
NX = 64
NY = 1024
N_GX = 8
N_GY = 4


def with_ends(drawn, own_key, low, top_value):
    longest = drawn.shape.index(max(drawn.shape))
    spots = []
    for shift in (0, 1):
        where = [jax.random.randint(jax.random.fold_in(own_key, axis), (), 0, length) for axis, length in enumerate(drawn.shape)]
        where[longest] = (where[longest] + shift) % drawn.shape[longest]
        spots.append(tuple(where))
    return drawn.at[spots[0]].set(low).at[spots[1]].set(top_value)


def block_scale(rng, dims, shards, low, high):
    factor_of, own = 1.0, jax.random.fold_in(rng, 6)
    for dim, parts in shards:
        heights = jnp.exp(jax.random.uniform(jax.random.fold_in(own, dim), (parts,), jnp.float32, low / len(shards), high / len(shards)))
        factor_of = factor_of * jnp.repeat(heights, dims[dim] // parts).reshape([-1 if axis == dim else 1 for axis in range(len(dims))])
    return factor_of


def assign_block(own_key, own, number, rows, number_of, top, reach, lean):
    ranking = jax.random.permutation(own_key, number_of)
    packed, ordinary = portions_of(number_of, rows * top, reach, lean, True), portions_of(number_of, rows * top, reach, lean, False)
    places = jnp.arange(number_of)

    def named(sizes, turn):
        used = int((sizes > 0).sum())
        fixed = max(1, used // 4)
        moved = fixed + (places - fixed + turn * (used - fixed)) % max(1, number_of - fixed)
        return jnp.zeros((number_of,), jnp.int32).at[ranking[jnp.where(places < fixed, places, moved)]].set(jnp.asarray(sizes, jnp.int32))

    sizes = jnp.where(number % 4 == 0, named(packed, number // 4), named(ordinary, number - number // 4 - 1))
    mixed = jax.random.permutation(jax.random.fold_in(own, 3), number_of)
    donor, sink = mixed[0:number_of // 2 * 2:2], mixed[1:number_of // 2 * 2:2]
    slack = jnp.minimum(sizes[donor] - 1, reach - sizes[sink]) // 2
    slack = jnp.where((donor == ranking[0]) | (sink == ranking[0]) | (sizes[sink] == 0), 0, jnp.maximum(slack, 0))
    moved = jax.random.randint(jax.random.fold_in(own, 4), (number_of // 2,), 0, 1 << 20) % (slack + 1)
    sizes = sizes.at[donor].add(-moved).at[sink].add(moved)
    items = jnp.searchsorted(jnp.cumsum(sizes), jnp.arange(rows * top), side="right").astype(jnp.int32)
    listing = items.reshape(top, rows).T
    listing = listing[jax.random.permutation(jax.random.fold_in(own, 1), rows)]
    turn = jax.random.randint(jax.random.fold_in(own, 2), (rows, 1), 0, top)
    return jnp.take_along_axis(listing, (jnp.arange(top)[None, :] + turn) % top, axis=1)


def portions_of(number_of, total, limit, lean, full):
    weights = [(1 << 20) // math.isqrt(rank ** lean) + 1 for rank in range(1, number_of + 1)]
    largest = limit if full else min(limit, max(-(-total // number_of), total * weights[0] // sum(weights)))
    least = 1 if total - largest >= number_of - 1 else 0
    counts, surplus = [largest] + [least] * (number_of - 1), total - largest - least * (number_of - 1)
    while surplus > 0:
        free = [i for i in range(1, number_of) if counts[i] < largest] or [i for i in range(1, number_of) if counts[i] < limit]
        pool, remaining = sum([weights[i] for i in free]), surplus
        for i in free:
            extra = min(limit - counts[i], max(1, remaining * weights[i] // pool), surplus)
            counts[i] = counts[i] + extra
            surplus = surplus - extra
    return np.array(counts)


def scatter_about(own_key, dims, scale, reach, split=(), dtype=jnp.bfloat16):
    gain = block_scale(own_key, dims, split, -0.22, 0.18) if split else 1.0
    result = jax.random.normal(own_key, dims, jnp.float32) * scale * gain
    return jnp.minimum(jnp.maximum(result, -reach), reach).astype(dtype)


def setup_inputs(seed: int = 0) -> dict:
    streams_of = jax.random.split(jax.random.key(seed), 9)
    rhs_field = scatter_about(streams_of[0], (2, NZ, NX, NY), 1.0, 6.0, ((2, 8), (3, 4)), jnp.float32)
    permittivity = jnp.clip(jnp.exp(math.log(4.0) - 1.3862944 * jax.random.uniform(streams_of[1], (NZ, NX, NY), jnp.float32) ** block_scale(streams_of[1], (NZ, NX, NY), ((1, 8), (2, 4)), -0.2, 0.2)), 1.0, 4.0)
    surf_dist = jnp.clip(0.2 + 0.8 * jax.random.uniform(streams_of[2], (NB, PTS), jnp.float32) ** block_scale(streams_of[2], (NB, PTS), ((0, 32),), -0.2, 0.2), 0.2, 1.0)
    surf_normal = scatter_about(streams_of[3], (3, NB, PTS), 1.0, 4.0, ((1, 32),), jnp.float32)
    surf_inc = scatter_about(streams_of[4], (2, NB, PTS), 1.0, 6.0, ((1, 32),), jnp.float32)
    surf_cell = with_ends(jax.random.randint(streams_of[5], (NB, PTS), 0, NZ * CX * CY), jax.random.fold_in(streams_of[5], 1), 0, (NZ * CX * CY) - 1).astype(jnp.int32)
    surf_mask = with_ends((jax.random.randint(streams_of[6], (NB, PTS), 0, 4) < 3).astype(jnp.int32), jax.random.fold_in(streams_of[6], 1), 0, 1)
    surf_owner_keys = jax.random.split(jax.random.fold_in(streams_of[7], 1), NB // SB)
    surf_owner_turns = jax.random.permutation(jax.random.fold_in(streams_of[7], 3), NB // SB)
    surf_owner = jax.vmap(lambda own, number: assign_block(jax.random.fold_in(streams_of[7], 2), own, number, SB, N_GX * N_GY, 1, CAP, 2))(surf_owner_keys, surf_owner_turns).reshape((NB, 1))
    return dict(rhs_field=rhs_field, permittivity=permittivity, surf_dist=surf_dist, surf_normal=surf_normal, surf_inc=surf_inc, surf_cell=surf_cell, surf_mask=surf_mask, surf_owner=surf_owner)


K_SQUARED = 0.25
BETA = 0.5
OMEGA = 0.8
TAU = 1.0


def apply_helm(padded, perm):
    center = padded[:, 1:-1, 1:-1, 1:-1]
    beside = padded[:, 2:, 1:-1, 1:-1] + padded[:, :-2, 1:-1, 1:-1]
    beside = beside + padded[:, 1:-1, 2:, 1:-1] + padded[:, 1:-1, :-2, 1:-1]
    beside = beside + padded[:, 1:-1, 1:-1, 2:] + padded[:, 1:-1, 1:-1, :-2]
    return (6.0 - K_SQUARED * perm)[None] * center - beside


def pad_all(field):
    return jnp.pad(field, ((0, 0), (1, 1), (1, 1), (1, 1)))


def reference(rhs_field, permittivity, surf_dist, surf_normal, surf_inc, surf_cell, surf_mask, surf_owner):
    owner_ids = jnp.broadcast_to(surf_owner, surf_cell.shape).reshape(-1)
    cells = surf_cell.reshape(-1)
    per_plane = CX * CY
    plane_idx = cells // per_plane
    remain = cells % per_plane
    row_idx = remain // CY + (owner_ids // N_GY) * CX
    col_idx = remain % CY + (owner_ids % N_GY) * CY
    stride_x = NY + 2
    stride_z = (NX + 2) * (NY + 2)
    pad_index = ((plane_idx + 1) * (NX + 2) + row_idx + 1) * stride_x + col_idx + 1
    grid_index = (plane_idx * NX + row_idx) * NY + col_idx
    weight = TAU * surf_mask.reshape(-1).astype(jnp.float32)
    dist = surf_dist.reshape(-1)
    normal = surf_normal.reshape(3, -1)
    incident = surf_inc.reshape(2, -1)

    diag_real = 6.0 - K_SQUARED * permittivity
    diag_imag = BETA * K_SQUARED * permittivity
    denom = diag_real * diag_real + diag_imag * diag_imag
    inv_real = diag_real / denom
    inv_imag = -diag_imag / denom

    def precond(vec):
        return jnp.stack([vec[0] * inv_real - vec[1] * inv_imag, vec[0] * inv_imag + vec[1] * inv_real])

    solution = jnp.zeros_like(rhs_field)
    residual = rhs_field
    for outer_no in range(ITERS):
        padded = pad_all(solution)
        image = apply_helm(padded, permittivity)
        flat_field = padded.reshape(2, -1)
        grad_dot = normal[0] * (flat_field[:, pad_index + stride_z] - flat_field[:, pad_index - stride_z])
        grad_dot = grad_dot + normal[1] * (flat_field[:, pad_index + stride_x] - flat_field[:, pad_index - stride_x])
        grad_dot = grad_dot + normal[2] * (flat_field[:, pad_index + 1] - flat_field[:, pad_index - 1])
        penalty = weight * (flat_field[:, pad_index] + dist * grad_dot * 0.5 + incident)
        surface = jnp.zeros((2, NZ * NX * NY), jnp.float32).at[:, grid_index].add(penalty)
        residual = rhs_field - image - surface.reshape(rhs_field.shape)
        update = OMEGA * precond(residual)
        for sweep_no in range(SWEEPS - 1):
            image_z = apply_helm(pad_all(update), permittivity)
            shifted = jnp.stack([image_z[0] - diag_imag * update[1], image_z[1] + diag_imag * update[0]])
            update = update + OMEGA * precond(residual - shifted)
        solution = solution + update
    return solution, residual
```

```python
import functools

import jax
import jax.numpy as jnp
from jax import lax
from jax.experimental import pallas as pl
from jax.experimental.pallas import tpu as pltpu
from jax.sharding import PartitionSpec as P

CAP = 2
K_SQUARED = 0.25
BETA = 0.5
OMEGA = 0.8
TAU = 1.0
FIELDS = 8
PARTS = 11
GROUP = 8
ROUNDS = 3
MESH = pl.DeviceIdType.MESH
F32 = jnp.float32
BF16 = jnp.bfloat16


def iota(shape, dim):
    return lax.broadcasted_iota(jnp.int32, shape, dim)


def kernel(
    n_gx, n_gy,
    rhs_ref, perm_ref, dist_ref, normal_ref, inc_ref, cell_ref, mask_ref, owner_ref,
    sol_ref, res_ref,
    send, recv, left, right, acc, row_send, row_recv, col_send, col_recv,
    block_out, block_in, halo_out, halo_in,
):
    gx, gy = lax.axis_index("gx"), lax.axis_index("gy")
    n = n_gx * n_gy
    me = gx * n_gy + gy
    blocks, points = cell_ref.shape
    planes, rows, cols = perm_ref.shape
    lines = planes * rows

    def peer(k):
        to = lax.rem(me + k, n)
        return to, (lax.div(to, n_gy), lax.rem(to, n_gy))

    barrier = pltpu.get_barrier_semaphore()

    def greet(k, carry):
        pl.semaphore_signal(barrier, inc=1, device_id=peer(k)[1], device_id_type=MESH)
        return carry

    lax.fori_loop(1, n, greet, 0)

    weight = TAU * mask_ref[...].astype(F32)
    half = weight * dist_ref[...] * 0.5
    data = jnp.concatenate(
        [
            cell_ref[...].astype(F32), weight,
            half * normal_ref[0], half * normal_ref[1], half * normal_ref[2],
            weight * inc_ref[0], weight * inc_ref[1],
            jnp.zeros((blocks, points), F32),
        ],
        axis=0,
    )
    wide = FIELDS * blocks
    lane_no = iota((blocks, wide), 1)
    lane_block = lane_no % blocks
    row_block = iota((blocks, wide), 0)
    owner = jnp.broadcast_to(owner_ref[...].astype(F32), (blocks, wide))
    owner_of = jnp.sum(jnp.where(row_block == lane_block, owner, 0.0), axis=0, keepdims=True)
    earlier = (owner == owner_of) & (row_block < lane_block)
    rank = jnp.sum(jnp.where(earlier, 1.0, 0.0), axis=0, keepdims=True)
    field_no = (iota((1, wide), 1) // blocks).astype(F32)
    target = (owner_of * CAP + rank) * FIELDS + field_no
    slots = n * CAP * FIELDS
    chosen = jnp.where(iota((slots, wide), 0).astype(F32) == target, 1.0, 0.0).astype(BF16)
    high = data.astype(BF16)
    rest = data - high.astype(F32)
    middle = rest.astype(BF16)
    low = (rest - middle.astype(F32)).astype(BF16)
    placed = jnp.dot(chosen, high, preferred_element_type=F32)
    placed = placed + jnp.dot(chosen, middle, preferred_element_type=F32)
    placed = placed + jnp.dot(chosen, low, preferred_element_type=F32)
    send[...] = placed.reshape(n, CAP * FIELDS, points)

    pl.semaphore_wait(barrier, n - 1)

    def block_copy(k):
        to, where = peer(k)
        return pltpu.make_async_remote_copy(
            src_ref=send.at[to], dst_ref=recv.at[k],
            send_sem=block_out.at[k], recv_sem=block_in.at[k],
            device_id=where, device_id_type=MESH,
        )

    def start_block(k, carry):
        block_copy(k).start()
        return carry

    lax.fori_loop(1, n, start_block, 0)
    recv[0] = send[me]

    @pl.when(gx == 0)
    def _():
        row_recv[:, 0] = jnp.zeros((ROUNDS, 2 * planes, cols), F32)

    @pl.when(gx == n_gx - 1)
    def _():
        row_recv[:, 1] = jnp.zeros((ROUNDS, 2 * planes, cols), F32)

    @pl.when(gy == 0)
    def _():
        col_recv[:, 0] = jnp.zeros((ROUNDS, 8, 2 * lines), F32)

    @pl.when(gy == n_gy - 1)
    def _():
        col_recv[:, 1] = jnp.zeros((ROUNDS, 8, 2 * lines), F32)

    perm = perm_ref[...]
    diag = 6.0 - K_SQUARED * perm
    shift = BETA * K_SQUARED * perm
    denom = diag * diag + shift * shift
    inv_real = diag / denom
    inv_imag = -shift / denom
    both_diag = jnp.concatenate([diag, diag], axis=0)

    acc[...] = jnp.zeros(acc.shape, F32)
    line_no = iota((lines, points), 0).astype(F32)
    col_no = iota((cols, points), 0).astype(F32)

    def gather_group(g, carry):
        for j in range(GROUP):
            k = g * GROUP + j

            @pl.when(k > 0)
            def _():
                block_copy(k).wait_recv()

        for j in range(GROUP):
            for r in range(CAP):
                tile = recv[g * GROUP + j, r * FIELDS:(r + 1) * FIELDS, :]
                at = slice((j * CAP + r) * points, (j * CAP + r + 1) * points)
                cell = tile[0:1]
                line = jnp.floor(cell * (1.0 / cols))
                column = cell - line * cols
                right[:, at] = jnp.where(col_no == column, 1.0, 0.0).astype(BF16)
                here = line_no == line
                left[0:lines, at] = jnp.where(here, tile[1:2], 0.0).astype(BF16)
                upper = tile.astype(BF16).astype(F32)
                lower = tile - upper
                for f in range(5):
                    for p, part in enumerate((upper, lower)):
                        top = (1 + 2 * f + p) * lines
                        value = jnp.where(here, part[2 + f:3 + f], 0.0)
                        left[top:top + lines, at] = value.astype(BF16)
        acc[...] += lax.dot_general(
            left[...], right[...], (((1,), (1,)), ((), ())), preferred_element_type=F32
        )
        return carry

    lax.fori_loop(0, n // GROUP, gather_group, 0)

    def summed(f):
        top = (1 + 2 * f) * lines
        both = acc[top:top + lines, :] + acc[top + lines:top + 2 * lines, :]
        return both.reshape(planes, rows, cols)

    def twice(x):
        return jnp.concatenate([x, x], axis=0)

    def precond(vec):
        real, imag = vec[:planes], vec[planes:]
        return jnp.concatenate(
            [real * inv_real - imag * inv_imag, real * inv_imag + imag * inv_real], axis=0
        )

    def halo_copies(step):
        out = []
        for side, (there, dx, dy) in enumerate(
            ((gx < n_gx - 1, 1, 0), (gx > 0, -1, 0), (gy < n_gy - 1, 0, 1), (gy > 0, 0, -1))
        ):
            source, sink = (row_send, row_recv) if side < 2 else (col_send, col_recv)
            out.append((there, pltpu.make_async_remote_copy(
                src_ref=source.at[step, side % 2], dst_ref=sink.at[step, side % 2],
                send_sem=halo_out.at[step, side], recv_sem=halo_in.at[step, side],
                device_id=(gx + dx, gy + dy), device_id_type=MESH,
            )))
        return out

    full = (2 * planes, rows, cols)
    row_at, col_at = iota(full, 1), iota(full, 2)

    def beside(step, v):
        flat = v.reshape(2 * lines, cols)
        row_send[step, 0] = v[:, rows - 1, :]
        row_send[step, 1] = v[:, 0, :]
        col_send[step, 0] = jnp.transpose(flat[:, cols - 128:])[120:128]
        col_send[step, 1] = jnp.transpose(flat[:, :128])[0:8]
        copies = halo_copies(step)
        for there, copy in copies:
            pl.when(there)(copy.start)
        zero = jnp.zeros((1, rows, cols), F32)
        z_next = jnp.concatenate([v[1:planes], zero, v[planes + 1:], zero], axis=0)
        z_last = jnp.concatenate([zero, v[:planes - 1], zero, v[planes:-1]], axis=0)
        x_next = pltpu.roll(v, rows - 1, 1)
        x_last = pltpu.roll(v, 1, 1)
        y_next = pltpu.roll(v, cols - 1, 2)
        y_last = pltpu.roll(v, 1, 2)
        for side, (there, copy) in enumerate(copies):
            comes = copies[side ^ 1][0]
            pl.when(comes)(copy.wait_recv)
            pl.when(there)(copy.wait_send)
        x_last = jnp.where(row_at == 0, row_recv[step, 0][:, None, :], x_last)
        x_next = jnp.where(row_at == rows - 1, row_recv[step, 1][:, None, :], x_next)

        def edge(row):
            column = jnp.transpose(jnp.broadcast_to(row, (2 * lines, 2 * lines)))
            return jnp.concatenate([column] * (cols // (2 * lines)), axis=1).reshape(full)

        y_last = jnp.where(col_at == 0, edge(col_recv[step, 0, 7:8, :]), y_last)
        y_next = jnp.where(col_at == cols - 1, edge(col_recv[step, 1, 0:1, :]), y_next)
        return z_next, z_last, x_next, x_last, y_next, y_last

    def helm(v, around):
        z_next, z_last, x_next, x_last, y_next, y_last = around
        return both_diag * v - (z_next + z_last + x_next + x_last + y_next + y_last)

    def sweep(step, z, residual):
        image = helm(z, beside(step, z))
        real = image[:planes] - shift * z[planes:]
        imag = image[planes:] + shift * z[:planes]
        return z + OMEGA * precond(residual - jnp.concatenate([real, imag], axis=0))

    source = rhs_ref[...] - jnp.concatenate([summed(3), summed(4)], axis=0)
    solution = sweep(0, OMEGA * precond(source), source)
    around = beside(1, solution)
    z_next, z_last, x_next, x_last, y_next, y_last = around
    surface = twice(acc[0:lines, :].reshape(planes, rows, cols)) * solution
    surface = surface + twice(summed(0)) * (z_next - z_last)
    surface = surface + twice(summed(1)) * (x_next - x_last)
    surface = surface + twice(summed(2)) * (y_next - y_last)
    residual = source - helm(solution, around) - surface
    res_ref[...] = residual
    sol_ref[...] = solution + sweep(2, OMEGA * precond(residual), residual)

    def finish_block(k, carry):
        block_copy(k).wait_send()
        return carry

    lax.fori_loop(1, n, finish_block, 0)


def per_device(
    n_gx, n_gy,
    rhs_field, permittivity, surf_dist, surf_normal, surf_inc, surf_cell, surf_mask, surf_owner,
):
    planes, rows, cols = permittivity.shape
    points = surf_cell.shape[1]
    n = n_gx * n_gy
    lines = planes * rows
    field = jax.ShapeDtypeStruct((2 * planes, rows, cols), F32)
    vmem = pl.BlockSpec(memory_space=pltpu.VMEM)
    deep = GROUP * CAP * points
    sol, res = pl.pallas_call(
        functools.partial(kernel, n_gx, n_gy),
        out_shape=(field, field),
        in_specs=[vmem] * 8,
        out_specs=(vmem, vmem),
        scratch_shapes=[
            pltpu.VMEM((n, CAP * FIELDS, points), F32),
            pltpu.VMEM((n, CAP * FIELDS, points), F32),
            pltpu.VMEM((PARTS * lines, deep), BF16),
            pltpu.VMEM((cols, deep), BF16),
            pltpu.VMEM((PARTS * lines, cols), F32),
            pltpu.VMEM((ROUNDS, 2, 2 * planes, cols), F32),
            pltpu.VMEM((ROUNDS, 2, 2 * planes, cols), F32),
            pltpu.VMEM((ROUNDS, 2, 8, 2 * lines), F32),
            pltpu.VMEM((ROUNDS, 2, 8, 2 * lines), F32),
            pltpu.SemaphoreType.DMA((n,)),
            pltpu.SemaphoreType.DMA((n,)),
            pltpu.SemaphoreType.DMA((ROUNDS, 4)),
            pltpu.SemaphoreType.DMA((ROUNDS, 4)),
        ],
        compiler_params=pltpu.CompilerParams(
            collective_id=0, has_side_effects=True, vmem_limit_bytes=48 * 1024 * 1024
        ),
    )(
        rhs_field.reshape(field.shape), permittivity, surf_dist, surf_normal, surf_inc,
        surf_cell, surf_mask, surf_owner,
    )
    return sol.reshape(rhs_field.shape), res.reshape(rhs_field.shape)


def solution(mesh):
    placed = (
        P(None, None, "gx", "gy"),
        P(None, "gx", "gy"),
        P(("gx", "gy"), None),
        P(None, ("gx", "gy"), None),
        P(None, ("gx", "gy"), None),
        P(("gx", "gy"), None),
        P(("gx", "gy"), None),
        P(("gx", "gy"), None),
    )
    return jax.shard_map(
        functools.partial(per_device, mesh.shape["gx"], mesh.shape["gy"]),
        mesh=mesh,
        in_specs=placed,
        out_specs=(P(None, None, "gx", "gy"), P(None, None, "gx", "gy")),
        check_vma=False,
    )
```

```python
import functools

import jax
import jax.numpy as jnp
from jax import lax
from jax.experimental import pallas as pl
from jax.experimental.pallas import tpu as pltpu
from jax.sharding import PartitionSpec as P

CAP = 2
K_SQUARED = 0.25
BETA = 0.5
OMEGA = 0.8
TAU = 1.0
FIELDS = 7
SENT = CAP * FIELDS
ROWS = -(-SENT // 8) * 8
PARTS = 11
GROUP = 8
ROUNDS = 3
MESH = pl.DeviceIdType.MESH
F32 = jnp.float32
BF16 = jnp.bfloat16


def iota(shape, dim):
    return lax.broadcasted_iota(jnp.int32, shape, dim)


def kernel(
    n_gx, n_gy,
    rhs_hbm, perm_hbm, dist_hbm, normal_hbm, inc_hbm, cell_hbm, mask_hbm, owner_hbm,
    sol_hbm, res_hbm,
    rhs_ref, perm_ref, dist_ref, normal_ref, inc_ref, cell_ref, mask_ref, owner_ref,
    send, recv, left, right, acc, row_send, row_recv, col_send, col_recv,
    sol_ref, res_ref, loaded, written, block_out, block_in, halo_out, halo_in,
):
    gx, gy = lax.axis_index("gx"), lax.axis_index("gy")
    n = n_gx * n_gy
    me = gx * n_gy + gy
    blocks, points = cell_ref.shape
    planes, rows, cols = perm_ref.shape
    lines = planes * rows

    def peer(k):
        to = lax.rem(me + k, n)
        return to, (lax.div(to, n_gy), lax.rem(to, n_gy))

    barrier = pltpu.get_barrier_semaphore()

    def greet(k, carry):
        pl.semaphore_signal(barrier, inc=1, device_id=peer(k)[1], device_id_type=MESH)
        return carry

    lax.fori_loop(1, n, greet, 0)
    loads = [
        pltpu.make_async_copy(source, sink, loaded.at[i])
        for i, (source, sink) in enumerate((
            (owner_hbm, owner_ref), (cell_hbm, cell_ref), (mask_hbm, mask_ref),
            (dist_hbm, dist_ref), (normal_hbm, normal_ref), (inc_hbm, inc_ref),
            (perm_hbm, perm_ref), (rhs_hbm, rhs_ref),
        ))
    ]
    for load in loads:
        load.start()
    for load in loads[:6]:
        load.wait()

    weight = TAU * mask_ref[...].astype(F32)
    half = weight * dist_ref[...] * 0.5
    data = jnp.concatenate(
        [
            cell_ref[...].astype(F32), weight,
            half * normal_ref[0], half * normal_ref[1], half * normal_ref[2],
            weight * inc_ref[0], weight * inc_ref[1],
        ],
        axis=0,
    )
    wide = FIELDS * blocks
    lane_no = iota((blocks, wide), 1)
    lane_block = lane_no % blocks
    row_block = iota((blocks, wide), 0)
    square = (blocks, blocks)
    owner = jnp.where(iota(square, 0) == iota(square, 1), owner_ref[...].astype(F32), 0.0)
    owner = jnp.broadcast_to(jnp.sum(owner, axis=1, keepdims=True), (blocks, wide))
    owner_of = jnp.sum(jnp.where(row_block == lane_block, owner, 0.0), axis=0, keepdims=True)
    earlier = (owner == owner_of) & (row_block < lane_block)
    rank = jnp.sum(jnp.where(earlier, 1.0, 0.0), axis=0, keepdims=True)
    field_no = (iota((1, wide), 1) // blocks).astype(F32)
    target = owner_of * ROWS + rank * FIELDS + field_no
    slots = n * ROWS
    chosen = jnp.where(iota((slots, wide), 0).astype(F32) == target, 1.0, 0.0).astype(BF16)
    high = data.astype(BF16)
    rest = data - high.astype(F32)
    middle = rest.astype(BF16)
    low = (rest - middle.astype(F32)).astype(BF16)
    placed = jnp.dot(chosen, high, preferred_element_type=F32)
    placed = placed + jnp.dot(chosen, middle, preferred_element_type=F32)
    placed = placed + jnp.dot(chosen, low, preferred_element_type=F32)
    send[...] = placed.reshape(n, ROWS, points)

    pl.semaphore_wait(barrier, n - 1)

    def block_copy(k):
        to, where = peer(k)
        return pltpu.make_async_remote_copy(
            src_ref=send.at[to, pl.ds(0, SENT)], dst_ref=recv.at[k, pl.ds(0, SENT)],
            send_sem=block_out.at[k], recv_sem=block_in.at[k],
            device_id=where, device_id_type=MESH,
        )

    def start_block(k, carry):
        block_copy(k).start()
        return carry

    lax.fori_loop(1, n, start_block, 0)
    recv[0] = send[me]
    for load in loads[6:]:
        load.wait()

    @pl.when(gx == 0)
    def _():
        row_recv[:, 0] = jnp.zeros((ROUNDS, 2 * planes, cols), F32)

    @pl.when(gx == n_gx - 1)
    def _():
        row_recv[:, 1] = jnp.zeros((ROUNDS, 2 * planes, cols), F32)

    @pl.when(gy == 0)
    def _():
        col_recv[:, 0] = jnp.zeros((ROUNDS, 8, 2 * lines), F32)

    @pl.when(gy == n_gy - 1)
    def _():
        col_recv[:, 1] = jnp.zeros((ROUNDS, 8, 2 * lines), F32)

    perm = perm_ref[...]
    diag = 6.0 - K_SQUARED * perm
    shift = BETA * K_SQUARED * perm
    denom = diag * diag + shift * shift
    inv_real = diag / denom
    inv_imag = -shift / denom
    both_diag = jnp.concatenate([diag, diag], axis=0)

    acc[...] = jnp.zeros(acc.shape, F32)
    line_no = iota((lines, points), 0).astype(F32)
    col_no = iota((cols, points), 0).astype(F32)

    def gather_group(g, carry):
        for j in range(GROUP):
            k = g * GROUP + j

            @pl.when(k > 0)
            def _():
                block_copy(k).wait_recv()

        for j in range(GROUP):
            for r in range(CAP):
                tile = recv[g * GROUP + j, r * FIELDS:(r + 1) * FIELDS, :]
                at = slice((j * CAP + r) * points, (j * CAP + r + 1) * points)
                cell = tile[0:1]
                line = jnp.floor(cell * (1.0 / cols))
                column = cell - line * cols
                right[:, at] = jnp.where(col_no == column, 1.0, 0.0).astype(BF16)
                here = line_no == line
                left[0:lines, at] = jnp.where(here, tile[1:2], 0.0).astype(BF16)
                upper = tile.astype(BF16).astype(F32)
                lower = tile - upper
                for f in range(5):
                    for p, part in enumerate((upper, lower)):
                        top = (1 + 2 * f + p) * lines
                        value = jnp.where(here, part[2 + f:3 + f], 0.0)
                        left[top:top + lines, at] = value.astype(BF16)
        acc[...] += lax.dot_general(
            left[...], right[...], (((1,), (1,)), ((), ())), preferred_element_type=F32
        )
        return carry

    lax.fori_loop(0, n // GROUP, gather_group, 0)

    def summed(f):
        top = (1 + 2 * f) * lines
        both = acc[top:top + lines, :] + acc[top + lines:top + 2 * lines, :]
        return both.reshape(planes, rows, cols)

    def twice(x):
        return jnp.concatenate([x, x], axis=0)

    def precond(vec):
        real, imag = vec[:planes], vec[planes:]
        return jnp.concatenate(
            [real * inv_real - imag * inv_imag, real * inv_imag + imag * inv_real], axis=0
        )

    def halo_copies(step):
        out = []
        for side, (there, dx, dy) in enumerate(
            ((gx < n_gx - 1, 1, 0), (gx > 0, -1, 0), (gy < n_gy - 1, 0, 1), (gy > 0, 0, -1))
        ):
            source, sink = (row_send, row_recv) if side < 2 else (col_send, col_recv)
            out.append((there, pltpu.make_async_remote_copy(
                src_ref=source.at[step, side % 2], dst_ref=sink.at[step, side % 2],
                send_sem=halo_out.at[step, side], recv_sem=halo_in.at[step, side],
                device_id=(gx + dx, gy + dy), device_id_type=MESH,
            )))
        return out

    full = (2 * planes, rows, cols)
    row_at, col_at = iota(full, 1), iota(full, 2)

    def beside(step, v):
        flat = v.reshape(2 * lines, cols)
        row_send[step, 0] = v[:, rows - 1, :]
        row_send[step, 1] = v[:, 0, :]
        col_send[step, 0] = jnp.transpose(flat[:, cols - 128:])[120:128]
        col_send[step, 1] = jnp.transpose(flat[:, :128])[0:8]
        copies = halo_copies(step)
        for there, copy in copies:
            pl.when(there)(copy.start)
        zero = jnp.zeros((1, rows, cols), F32)
        z_next = jnp.concatenate([v[1:planes], zero, v[planes + 1:], zero], axis=0)
        z_last = jnp.concatenate([zero, v[:planes - 1], zero, v[planes:-1]], axis=0)
        x_next = pltpu.roll(v, rows - 1, 1)
        x_last = pltpu.roll(v, 1, 1)
        y_next = pltpu.roll(v, cols - 1, 2)
        y_last = pltpu.roll(v, 1, 2)
        for side, (there, copy) in enumerate(copies):
            comes = copies[side ^ 1][0]
            pl.when(comes)(copy.wait_recv)
            pl.when(there)(copy.wait_send)
        x_last = jnp.where(row_at == 0, row_recv[step, 0][:, None, :], x_last)
        x_next = jnp.where(row_at == rows - 1, row_recv[step, 1][:, None, :], x_next)

        def edge(row):
            column = jnp.transpose(jnp.broadcast_to(row, (2 * lines, 2 * lines)))
            return jnp.concatenate([column] * (cols // (2 * lines)), axis=1).reshape(full)

        y_last = jnp.where(col_at == 0, edge(col_recv[step, 0, 7:8, :]), y_last)
        y_next = jnp.where(col_at == cols - 1, edge(col_recv[step, 1, 0:1, :]), y_next)
        return z_next, z_last, x_next, x_last, y_next, y_last

    def helm(v, around):
        z_next, z_last, x_next, x_last, y_next, y_last = around
        return both_diag * v - (z_next + z_last + x_next + x_last + y_next + y_last)

    def sweep(step, z, residual):
        image = helm(z, beside(step, z))
        real = image[:planes] - shift * z[planes:]
        imag = image[planes:] + shift * z[:planes]
        return z + OMEGA * precond(residual - jnp.concatenate([real, imag], axis=0))

    source = rhs_ref[...] - jnp.concatenate([summed(3), summed(4)], axis=0)
    solution = sweep(0, OMEGA * precond(source), source)
    around = beside(1, solution)
    z_next, z_last, x_next, x_last, y_next, y_last = around
    surface = twice(acc[0:lines, :].reshape(planes, rows, cols)) * solution
    surface = surface + twice(summed(0)) * (z_next - z_last)
    surface = surface + twice(summed(1)) * (x_next - x_last)
    surface = surface + twice(summed(2)) * (y_next - y_last)
    residual = source - helm(solution, around) - surface
    res_ref[...] = residual
    res_write = pltpu.make_async_copy(res_ref, res_hbm, written.at[0])
    res_write.start()
    sol_ref[...] = solution + sweep(2, OMEGA * precond(residual), residual)
    sol_write = pltpu.make_async_copy(sol_ref, sol_hbm, written.at[1])
    sol_write.start()

    def finish_block(k, carry):
        block_copy(k).wait_send()
        return carry

    lax.fori_loop(1, n, finish_block, 0)
    res_write.wait()
    sol_write.wait()


def write_out(sol_ref, res_ref, sol_hbm, res_hbm, done):
    copies = (
        pltpu.make_async_copy(sol_ref, sol_hbm, done.at[0]),
        pltpu.make_async_copy(res_ref, res_hbm, done.at[1]),
    )
    for copy in copies:
        copy.start()
    for copy in copies:
        copy.wait()


def per_device(
    n_gx, n_gy,
    rhs_field, permittivity, surf_dist, surf_normal, surf_inc, surf_cell, surf_mask, surf_owner,
):
    planes, rows, cols = permittivity.shape
    points = surf_cell.shape[1]
    n = n_gx * n_gy
    lines = planes * rows
    field = jax.ShapeDtypeStruct((2 * planes, rows, cols), F32)
    hbm = pl.BlockSpec(memory_space=pltpu.HBM)
    owner = surf_owner.reshape(1, -1)
    operands = (
        rhs_field.reshape(field.shape), permittivity, surf_dist, surf_normal, surf_inc,
        surf_cell, surf_mask, owner,
    )
    deep = GROUP * CAP * points
    sol, res = pl.pallas_call(
        functools.partial(kernel, n_gx, n_gy),
        out_shape=(field, field),
        in_specs=[hbm] * 8,
        out_specs=(hbm, hbm),
        scratch_shapes=[
            *[pltpu.VMEM(x.shape, x.dtype) for x in operands],
            pltpu.VMEM((n, ROWS, points), F32),
            pltpu.VMEM((n, ROWS, points), F32),
            pltpu.VMEM((PARTS * lines, deep), BF16),
            pltpu.VMEM((cols, deep), BF16),
            pltpu.VMEM((PARTS * lines, cols), F32),
            pltpu.VMEM((ROUNDS, 2, 2 * planes, cols), F32),
            pltpu.VMEM((ROUNDS, 2, 2 * planes, cols), F32),
            pltpu.VMEM((ROUNDS, 2, 8, 2 * lines), F32),
            pltpu.VMEM((ROUNDS, 2, 8, 2 * lines), F32),
            pltpu.VMEM(field.shape, F32),
            pltpu.VMEM(field.shape, F32),
            pltpu.SemaphoreType.DMA((8,)),
            pltpu.SemaphoreType.DMA((2,)),
            pltpu.SemaphoreType.DMA((n,)),
            pltpu.SemaphoreType.DMA((n,)),
            pltpu.SemaphoreType.DMA((ROUNDS, 4)),
            pltpu.SemaphoreType.DMA((ROUNDS, 4)),
        ],
        compiler_params=pltpu.CompilerParams(
            collective_id=0, has_side_effects=True, vmem_limit_bytes=64 * 1024 * 1024
        ),
    )(*operands)
    sol, res = pl.pallas_call(
        write_out,
        out_shape=(field, field),
        in_specs=[hbm] * 2,
        out_specs=(hbm, hbm),
        scratch_shapes=[pltpu.SemaphoreType.DMA((2,))],
        compiler_params=pltpu.CompilerParams(vmem_limit_bytes=64 * 1024 * 1024),
    )(sol, res)
    return sol.reshape(rhs_field.shape), res.reshape(rhs_field.shape)


def solution(mesh):
    placed = (
        P(None, None, "gx", "gy"),
        P(None, "gx", "gy"),
        P(("gx", "gy"), None),
        P(None, ("gx", "gy"), None),
        P(None, ("gx", "gy"), None),
        P(("gx", "gy"), None),
        P(("gx", "gy"), None),
        P(("gx", "gy"), None),
    )
    return jax.shard_map(
        functools.partial(per_device, mesh.shape["gx"], mesh.shape["gy"]),
        mesh=mesh,
        in_specs=placed,
        out_specs=(P(None, None, "gx", "gy"), P(None, None, "gx", "gy")),
        check_vma=False,
    )
```

```python
import functools

import jax
import jax.numpy as jnp
from jax import lax
from jax.experimental import pallas as pl
from jax.experimental.pallas import tpu as pltpu
from jax.sharding import PartitionSpec as P

CAP = 2
K_SQUARED = 0.25
BETA = 0.5
OMEGA = 0.8
TAU = 1.0
FIELDS = 7
SENT = CAP * FIELDS
ROWS = -(-SENT // 8) * 8
PARTS = 11
GROUP = 8
ROUNDS = 3
MESH = pl.DeviceIdType.MESH
F32 = jnp.float32
BF16 = jnp.bfloat16


def iota(shape, dim):
    return lax.broadcasted_iota(jnp.int32, shape, dim)


def kernel(
    n_gx, n_gy,
    rhs_hbm, perm_hbm, dist_hbm, normal_hbm, inc_hbm, cell_hbm, mask_hbm, owner_hbm,
    sol_hbm, res_hbm,
    rhs_ref, perm_ref, dist_ref, normal_ref, inc_ref, cell_ref, mask_ref, owner_ref,
    send, recv, left, right, acc, row_send, row_recv, col_send, col_recv,
    sol_ref, res_ref, loaded, written, block_out, block_in, halo_out, halo_in,
):
    gx, gy = lax.axis_index("gx"), lax.axis_index("gy")
    n = n_gx * n_gy
    me = gx * n_gy + gy
    blocks, points = cell_ref.shape
    planes, rows, cols = perm_ref.shape
    lines = planes * rows

    def peer(k):
        to = lax.rem(me + k, n)
        return to, (lax.div(to, n_gy), lax.rem(to, n_gy))

    barrier = pltpu.get_barrier_semaphore()

    def greet(k, carry):
        pl.semaphore_signal(barrier, inc=1, device_id=peer(k)[1], device_id_type=MESH)
        return carry

    lax.fori_loop(1, n, greet, 0)
    loads = [
        pltpu.make_async_copy(source, sink, loaded.at[i])
        for i, (source, sink) in enumerate((
            (owner_hbm, owner_ref), (cell_hbm, cell_ref), (mask_hbm, mask_ref),
            (dist_hbm, dist_ref), (normal_hbm, normal_ref), (inc_hbm, inc_ref),
            (perm_hbm, perm_ref), (rhs_hbm, rhs_ref),
        ))
    ]
    for load in loads:
        load.start()
    for load in loads[:6]:
        load.wait()

    weight = TAU * mask_ref[...].astype(F32)
    half = weight * dist_ref[...] * 0.5
    data = jnp.concatenate(
        [
            cell_ref[...].astype(F32), weight,
            half * normal_ref[0], half * normal_ref[1], half * normal_ref[2],
            weight * inc_ref[0], weight * inc_ref[1],
        ],
        axis=0,
    )
    wide = FIELDS * blocks
    lane_no = iota((blocks, wide), 1)
    lane_block = lane_no % blocks
    row_block = iota((blocks, wide), 0)
    square = (blocks, blocks)
    owner = jnp.where(iota(square, 0) == iota(square, 1), owner_ref[...].astype(F32), 0.0)
    owner = jnp.broadcast_to(jnp.sum(owner, axis=1, keepdims=True), (blocks, wide))
    owner_of = jnp.sum(jnp.where(row_block == lane_block, owner, 0.0), axis=0, keepdims=True)
    earlier = (owner == owner_of) & (row_block < lane_block)
    rank = jnp.sum(jnp.where(earlier, 1.0, 0.0), axis=0, keepdims=True)
    field_no = (iota((1, wide), 1) // blocks).astype(F32)
    target = owner_of * ROWS + rank * FIELDS + field_no
    slots = n * ROWS
    chosen = jnp.where(iota((slots, wide), 0).astype(F32) == target, 1.0, 0.0).astype(BF16)
    high = data.astype(BF16)
    rest = data - high.astype(F32)
    middle = rest.astype(BF16)
    low = (rest - middle.astype(F32)).astype(BF16)
    placed = jnp.dot(chosen, high, preferred_element_type=F32)
    placed = placed + jnp.dot(chosen, middle, preferred_element_type=F32)
    placed = placed + jnp.dot(chosen, low, preferred_element_type=F32)
    send[...] = placed.reshape(n, ROWS, points)

    pl.semaphore_wait(barrier, n - 1)

    def block_copy(k):
        to, where = peer(k)
        return pltpu.make_async_remote_copy(
            src_ref=send.at[to, pl.ds(0, SENT)], dst_ref=recv.at[k, pl.ds(0, SENT)],
            send_sem=block_out.at[k], recv_sem=block_in.at[k],
            device_id=where, device_id_type=MESH,
        )

    def start_block(k, carry):
        block_copy(k).start()
        return carry

    lax.fori_loop(1, n, start_block, 0)
    recv[0] = send[me]
    for load in loads[6:]:
        load.wait()

    @pl.when(gx == 0)
    def _():
        row_recv[:, 0] = jnp.zeros((ROUNDS, 2 * planes, cols), F32)

    @pl.when(gx == n_gx - 1)
    def _():
        row_recv[:, 1] = jnp.zeros((ROUNDS, 2 * planes, cols), F32)

    @pl.when(gy == 0)
    def _():
        col_recv[:, 0] = jnp.zeros((ROUNDS, 8, 2 * lines), F32)

    @pl.when(gy == n_gy - 1)
    def _():
        col_recv[:, 1] = jnp.zeros((ROUNDS, 8, 2 * lines), F32)

    perm = perm_ref[...]
    diag = 6.0 - K_SQUARED * perm
    shift = BETA * K_SQUARED * perm
    denom = diag * diag + shift * shift
    inv_real = diag / denom
    inv_imag = -shift / denom
    both_diag = jnp.concatenate([diag, diag], axis=0)

    acc[...] = jnp.zeros(acc.shape, F32)
    line_no = iota((lines, points), 0).astype(F32)
    col_no = iota((cols, points), 0).astype(F32)

    def gather_group(g, carry):
        for j in range(GROUP):
            k = g * GROUP + j

            @pl.when(k > 0)
            def _():
                block_copy(k).wait_recv()

        for j in range(GROUP):
            for r in range(CAP):
                tile = recv[g * GROUP + j, r * FIELDS:(r + 1) * FIELDS, :]
                at = slice((j * CAP + r) * points, (j * CAP + r + 1) * points)
                cell = tile[0:1]
                line = jnp.floor(cell * (1.0 / cols))
                column = cell - line * cols
                right[:, at] = jnp.where(col_no == column, 1.0, 0.0).astype(BF16)
                here = line_no == line
                left[0:lines, at] = jnp.where(here, tile[1:2], 0.0).astype(BF16)
                upper = tile.astype(BF16).astype(F32)
                lower = tile - upper
                for f in range(5):
                    for p, part in enumerate((upper, lower)):
                        top = (1 + 2 * f + p) * lines
                        value = jnp.where(here, part[2 + f:3 + f], 0.0)
                        left[top:top + lines, at] = value.astype(BF16)
        acc[...] += lax.dot_general(
            left[...], right[...], (((1,), (1,)), ((), ())), preferred_element_type=F32
        )
        return carry

    lax.fori_loop(0, n // GROUP, gather_group, 0)

    def summed(f):
        top = (1 + 2 * f) * lines
        both = acc[top:top + lines, :] + acc[top + lines:top + 2 * lines, :]
        return both.reshape(planes, rows, cols)

    def twice(x):
        return jnp.concatenate([x, x], axis=0)

    def precond(vec):
        real, imag = vec[:planes], vec[planes:]
        return jnp.concatenate(
            [real * inv_real - imag * inv_imag, real * inv_imag + imag * inv_real], axis=0
        )

    def halo_copies(step):
        out = []
        for side, (there, dx, dy) in enumerate(
            ((gx < n_gx - 1, 1, 0), (gx > 0, -1, 0), (gy < n_gy - 1, 0, 1), (gy > 0, 0, -1))
        ):
            source, sink = (row_send, row_recv) if side < 2 else (col_send, col_recv)
            out.append((there, pltpu.make_async_remote_copy(
                src_ref=source.at[step, side % 2], dst_ref=sink.at[step, side % 2],
                send_sem=halo_out.at[step, side], recv_sem=halo_in.at[step, side],
                device_id=(gx + dx, gy + dy), device_id_type=MESH,
            )))
        return out

    full = (2 * planes, rows, cols)
    row_at, col_at = iota(full, 1), iota(full, 2)

    def beside(step, v):
        flat = v.reshape(2 * lines, cols)
        row_send[step, 0] = v[:, rows - 1, :]
        row_send[step, 1] = v[:, 0, :]
        col_send[step, 0] = jnp.transpose(flat[:, cols - 128:])[120:128]
        col_send[step, 1] = jnp.transpose(flat[:, :128])[0:8]
        copies = halo_copies(step)
        for there, copy in copies:
            pl.when(there)(copy.start)
        zero = jnp.zeros((1, rows, cols), F32)
        z_next = jnp.concatenate([v[1:planes], zero, v[planes + 1:], zero], axis=0)
        z_last = jnp.concatenate([zero, v[:planes - 1], zero, v[planes:-1]], axis=0)
        x_next = pltpu.roll(v, rows - 1, 1)
        x_last = pltpu.roll(v, 1, 1)
        y_next = pltpu.roll(v, cols - 1, 2)
        y_last = pltpu.roll(v, 1, 2)
        for side, (there, copy) in enumerate(copies):
            comes = copies[side ^ 1][0]
            pl.when(comes)(copy.wait_recv)
            pl.when(there)(copy.wait_send)
        x_last = jnp.where(row_at == 0, row_recv[step, 0][:, None, :], x_last)
        x_next = jnp.where(row_at == rows - 1, row_recv[step, 1][:, None, :], x_next)

        def edge(row):
            column = jnp.transpose(jnp.broadcast_to(row, (2 * lines, 2 * lines)))
            return jnp.concatenate([column] * (cols // (2 * lines)), axis=1).reshape(full)

        y_last = jnp.where(col_at == 0, edge(col_recv[step, 0, 7:8, :]), y_last)
        y_next = jnp.where(col_at == cols - 1, edge(col_recv[step, 1, 0:1, :]), y_next)
        return z_next, z_last, x_next, x_last, y_next, y_last

    def helm(v, around):
        z_next, z_last, x_next, x_last, y_next, y_last = around
        return both_diag * v - (z_next + z_last + x_next + x_last + y_next + y_last)

    def sweep(step, z, residual):
        image = helm(z, beside(step, z))
        real = image[:planes] - shift * z[planes:]
        imag = image[planes:] + shift * z[:planes]
        return z + OMEGA * precond(residual - jnp.concatenate([real, imag], axis=0))

    source = rhs_ref[...] - jnp.concatenate([summed(3), summed(4)], axis=0)
    solution = sweep(0, OMEGA * precond(source), source)
    around = beside(1, solution)
    z_next, z_last, x_next, x_last, y_next, y_last = around
    surface = twice(acc[0:lines, :].reshape(planes, rows, cols)) * solution
    surface = surface + twice(summed(0)) * (z_next - z_last)
    surface = surface + twice(summed(1)) * (x_next - x_last)
    surface = surface + twice(summed(2)) * (y_next - y_last)
    residual = source - helm(solution, around) - surface
    res_ref[...] = residual
    res_write = pltpu.make_async_copy(res_ref, res_hbm, written.at[0])
    res_write.start()
    sol_ref[...] = solution + sweep(2, OMEGA * precond(residual), residual)
    sol_write = pltpu.make_async_copy(sol_ref, sol_hbm, written.at[1])
    sol_write.start()

    def finish_block(k, carry):
        block_copy(k).wait_send()
        return carry

    lax.fori_loop(1, n, finish_block, 0)
    res_write.wait()
    sol_write.wait()


def write_out(sol_ref, res_ref, sol_out, res_out, sol_held, res_held, here, done):
    loads = (
        pltpu.make_async_copy(sol_ref, sol_held, here.at[0]),
        pltpu.make_async_copy(res_ref, res_held, here.at[1]),
    )
    stores = (
        pltpu.make_async_copy(sol_held, sol_out, done.at[0]),
        pltpu.make_async_copy(res_held, res_out, done.at[1]),
    )
    for load in loads:
        load.start()
    for load, store in zip(loads, stores):
        load.wait()
        store.start()
    for store in stores:
        store.wait()


def per_device(
    n_gx, n_gy,
    rhs_field, permittivity, surf_dist, surf_normal, surf_inc, surf_cell, surf_mask, surf_owner,
):
    planes, rows, cols = permittivity.shape
    points = surf_cell.shape[1]
    n = n_gx * n_gy
    lines = planes * rows
    field = jax.ShapeDtypeStruct((2 * planes, rows, cols), F32)
    hbm = pl.BlockSpec(memory_space=pltpu.HBM)
    owner = surf_owner.reshape(1, -1)
    operands = (
        rhs_field.reshape(field.shape), permittivity, surf_dist, surf_normal, surf_inc,
        surf_cell, surf_mask, owner,
    )
    deep = GROUP * CAP * points
    sol, res = pl.pallas_call(
        functools.partial(kernel, n_gx, n_gy),
        out_shape=(field, field),
        in_specs=[hbm] * 8,
        out_specs=(hbm, hbm),
        scratch_shapes=[
            *[pltpu.VMEM(x.shape, x.dtype) for x in operands],
            pltpu.VMEM((n, ROWS, points), F32),
            pltpu.VMEM((n, ROWS, points), F32),
            pltpu.VMEM((PARTS * lines, deep), BF16),
            pltpu.VMEM((cols, deep), BF16),
            pltpu.VMEM((PARTS * lines, cols), F32),
            pltpu.VMEM((ROUNDS, 2, 2 * planes, cols), F32),
            pltpu.VMEM((ROUNDS, 2, 2 * planes, cols), F32),
            pltpu.VMEM((ROUNDS, 2, 8, 2 * lines), F32),
            pltpu.VMEM((ROUNDS, 2, 8, 2 * lines), F32),
            pltpu.VMEM(field.shape, F32),
            pltpu.VMEM(field.shape, F32),
            pltpu.SemaphoreType.DMA((8,)),
            pltpu.SemaphoreType.DMA((2,)),
            pltpu.SemaphoreType.DMA((n,)),
            pltpu.SemaphoreType.DMA((n,)),
            pltpu.SemaphoreType.DMA((ROUNDS, 4)),
            pltpu.SemaphoreType.DMA((ROUNDS, 4)),
        ],
        compiler_params=pltpu.CompilerParams(
            collective_id=0, has_side_effects=True, vmem_limit_bytes=64 * 1024 * 1024
        ),
    )(*operands)
    sol, res = pl.pallas_call(
        write_out,
        out_shape=(field, field),
        in_specs=[hbm] * 2,
        out_specs=(hbm, hbm),
        scratch_shapes=[
            pltpu.VMEM(field.shape, F32),
            pltpu.VMEM(field.shape, F32),
            pltpu.SemaphoreType.DMA((2,)),
            pltpu.SemaphoreType.DMA((2,)),
        ],
        compiler_params=pltpu.CompilerParams(vmem_limit_bytes=64 * 1024 * 1024),
    )(sol, res)
    return sol.reshape(rhs_field.shape), res.reshape(rhs_field.shape)


def solution(mesh):
    placed = (
        P(None, None, "gx", "gy"),
        P(None, "gx", "gy"),
        P(("gx", "gy"), None),
        P(None, ("gx", "gy"), None),
        P(None, ("gx", "gy"), None),
        P(("gx", "gy"), None),
        P(("gx", "gy"), None),
        P(("gx", "gy"), None),
    )
    return jax.shard_map(
        functools.partial(per_device, mesh.shape["gx"], mesh.shape["gy"]),
        mesh=mesh,
        in_specs=placed,
        out_specs=(P(None, None, "gx", "gy"), P(None, None, "gx", "gy")),
        check_vma=False,
    )
```

```python
import functools

import jax
import jax.numpy as jnp
from jax import lax
from jax.experimental import pallas as pl
from jax.experimental.pallas import tpu as pltpu
from jax.sharding import PartitionSpec as P

CAP = 2
K_SQUARED = 0.25
BETA = 0.5
OMEGA = 0.8
TAU = 1.0
FIELDS = 7
SENT = CAP * FIELDS
ROWS = -(-SENT // 8) * 8
PARTS = 11
GROUP = 8
REACH = 3
MESH = pl.DeviceIdType.MESH
F32 = jnp.float32
BF16 = jnp.bfloat16


def iota(shape, dim):
    return lax.broadcasted_iota(jnp.int32, shape, dim)


def kernel(
    n_gx, n_gy,
    rhs_hbm, perm_hbm, dist_hbm, normal_hbm, inc_hbm, cell_hbm, mask_hbm, owner_hbm,
    sol_hbm, res_hbm,
    rhs_ref, perm_ref, dist_ref, normal_ref, inc_ref, cell_ref, mask_ref, owner_ref,
    send, recv, left, right, acc, right_ref, right_row, slope_ref, slope_row, perm_row, strip_send, strip_recv,
    sol_ref, res_ref, loaded, written, block_out, block_in, halo_out, halo_in,
):
    gx, gy = lax.axis_index("gx"), lax.axis_index("gy")
    n = n_gx * n_gy
    me = gx * n_gy + gy
    blocks, points = cell_ref.shape
    planes, rows, cols = perm_ref.shape
    lines = planes * rows

    def peer(k):
        to = lax.rem(me + k, n)
        return to, (lax.div(to, n_gy), lax.rem(to, n_gy))

    barrier = pltpu.get_barrier_semaphore()

    def greet(k, carry):
        pl.semaphore_signal(barrier, inc=1, device_id=peer(k)[1], device_id_type=MESH)
        return carry

    lax.fori_loop(1, n, greet, 0)
    loads = [
        pltpu.make_async_copy(source, sink, loaded.at[i])
        for i, (source, sink) in enumerate((
            (owner_hbm, owner_ref), (cell_hbm, cell_ref), (mask_hbm, mask_ref),
            (dist_hbm, dist_ref), (normal_hbm, normal_ref), (inc_hbm, inc_ref),
            (perm_hbm, perm_ref), (rhs_hbm, rhs_ref),
        ))
    ]
    for load in loads:
        load.start()
    for load in loads[:6]:
        load.wait()

    weight = TAU * mask_ref[...].astype(F32)
    half = weight * dist_ref[...] * 0.5
    data = jnp.concatenate(
        [
            cell_ref[...].astype(F32), weight,
            half * normal_ref[0], half * normal_ref[1], half * normal_ref[2],
            weight * inc_ref[0], weight * inc_ref[1],
        ],
        axis=0,
    )
    wide = FIELDS * blocks
    lane_no = iota((blocks, wide), 1)
    lane_block = lane_no % blocks
    row_block = iota((blocks, wide), 0)
    square = (blocks, blocks)
    owner = jnp.where(iota(square, 0) == iota(square, 1), owner_ref[...].astype(F32), 0.0)
    owner = jnp.broadcast_to(jnp.sum(owner, axis=1, keepdims=True), (blocks, wide))
    owner_of = jnp.sum(jnp.where(row_block == lane_block, owner, 0.0), axis=0, keepdims=True)
    earlier = (owner == owner_of) & (row_block < lane_block)
    rank = jnp.sum(jnp.where(earlier, 1.0, 0.0), axis=0, keepdims=True)
    field_no = (iota((1, wide), 1) // blocks).astype(F32)
    target = owner_of * ROWS + rank * FIELDS + field_no
    slots = n * ROWS
    chosen = jnp.where(iota((slots, wide), 0).astype(F32) == target, 1.0, 0.0).astype(BF16)
    high = data.astype(BF16)
    rest = data - high.astype(F32)
    middle = rest.astype(BF16)
    low = (rest - middle.astype(F32)).astype(BF16)
    placed = jnp.dot(chosen, high, preferred_element_type=F32)
    placed = placed + jnp.dot(chosen, middle, preferred_element_type=F32)
    placed = placed + jnp.dot(chosen, low, preferred_element_type=F32)
    send[...] = placed.reshape(n, ROWS, points)

    pl.semaphore_wait(barrier, n - 1)

    def block_copy(k):
        to, where = peer(k)
        return pltpu.make_async_remote_copy(
            src_ref=send.at[to, pl.ds(0, SENT)], dst_ref=recv.at[k, pl.ds(0, SENT)],
            send_sem=block_out.at[k], recv_sem=block_in.at[k],
            device_id=where, device_id_type=MESH,
        )

    def start_block(k, carry):
        block_copy(k).start()
        return carry

    lax.fori_loop(1, n, start_block, 0)
    recv[0] = send[me]
    for load in loads[6:]:
        load.wait()

    def within(x, y):
        return (x >= 0) & (x < n_gx) & (y >= 0) & (y < n_gy)

    def strips(first, field):
        flat = field.reshape(2 * lines, cols)
        strip_send[0, first] = jnp.transpose(flat[:, cols - 128:])[120:128]
        strip_send[1, first] = jnp.transpose(flat[:, :128])[0:8]

    def edge_copies(early):
        moves = []
        for side, dx in enumerate((1, -1)):
            top = rows - REACH if dx == 1 else 0
            end = rows - 1 if dx == 1 else 0
            if early:
                moves.append((dx, 0, perm_ref.at[:, pl.ds(top, REACH)], perm_row.at[:, pl.ds(top, REACH)]))
            else:
                moves.append((dx, 0, right_ref.at[:, pl.ds(top, REACH)], right_row.at[:, pl.ds(top, REACH)]))
                moves.append((dx, 0, slope_ref.at[:, pl.ds(end, 1)], slope_row.at[:, pl.ds(end, 1)]))
        part = pl.ds(0, 1) if early else pl.ds(1, 3)
        for side, dy in enumerate((1, -1)):
            for dx in (-1, 0, 1):
                moves.append((dx, dy, strip_send.at[side, part], strip_recv.at[side, dx + 1, part]))
        out = []
        for number, (dx, dy, source, sink) in enumerate(moves):
            which = (0 if early else 1, number)
            out.append((
                within(gx + dx, gy + dy), within(gx - dx, gy - dy),
                pltpu.make_async_remote_copy(
                    src_ref=source, dst_ref=sink,
                    send_sem=halo_out.at[which], recv_sem=halo_in.at[which],
                    device_id=(gx + dx, gy + dy), device_id_type=MESH,
                ),
            ))
        return out

    def start_edges(copies):
        for there, _, copy in copies:
            pl.when(there)(copy.start)

    def finish_edges(copies):
        for there, comes, copy in copies:
            pl.when(comes)(copy.wait_recv)

    def beside_tile(dx, first):
        empty = jnp.zeros((112, 2 * lines), F32)
        stacked = jnp.concatenate(
            [strip_recv[1, dx + 1, first], empty, strip_recv[0, dx + 1, first]], axis=0
        )
        return jnp.transpose(stacked).reshape(2 * planes, rows, 128)

    size = (2 * planes, rows, cols + 128)
    row_at, col_at = iota(size, 1), iota(size, 2)
    other = iota(size, 0) >= planes
    row_own = jnp.where(other, jnp.where(row_at < 4, rows + row_at, row_at - rows), row_at)
    col_own = jnp.where(col_at < cols + 64, col_at, col_at - (cols + 128))
    row_all, col_all = gx * rows + row_own, gy * cols + col_own
    inside = (row_all >= 0) & (row_all < n_gx * rows) & (col_all >= 0) & (col_all < n_gy * cols)
    valid = inside & (row_own >= -REACH) & (row_own < rows + REACH)

    def extended(own, around, first, part, corners=True):
        at = slice(part * planes, (part + 1) * planes)
        side = beside_tile(0, first)[at]
        if corners:
            near = iota((planes, rows, 128), 1) < 4
            far = jnp.where(near, beside_tile(-1, first)[at], beside_tile(1, first)[at])
        else:
            far = jnp.zeros(side.shape, F32)
        return jnp.concatenate([
            jnp.concatenate([own, side], axis=2), jnp.concatenate([around, far], axis=2)
        ], axis=0)

    strips(0, jnp.concatenate([perm_ref[...], perm_ref[...]], axis=0))
    early_copies = edge_copies(True)
    start_edges(early_copies)

    acc[...] = jnp.zeros(acc.shape, F32)
    line_no = iota((lines, points), 0).astype(F32)
    col_no = iota((cols, points), 0).astype(F32)

    def gather_group(g, carry):
        for j in range(GROUP):
            k = g * GROUP + j

            @pl.when(k > 0)
            def _():
                block_copy(k).wait_recv()

        for j in range(GROUP):
            for r in range(CAP):
                tile = recv[g * GROUP + j, r * FIELDS:(r + 1) * FIELDS, :]
                at = slice((j * CAP + r) * points, (j * CAP + r + 1) * points)
                cell = tile[0:1]
                line = jnp.floor(cell * (1.0 / cols))
                column = cell - line * cols
                right[:, at] = jnp.where(col_no == column, 1.0, 0.0).astype(BF16)
                here = line_no == line
                left[0:lines, at] = jnp.where(here, tile[1:2], 0.0).astype(BF16)
                upper = tile.astype(BF16).astype(F32)
                lower = tile - upper
                for f in range(5):
                    for p, part in enumerate((upper, lower)):
                        top = (1 + 2 * f + p) * lines
                        value = jnp.where(here, part[2 + f:3 + f], 0.0)
                        left[top:top + lines, at] = value.astype(BF16)
        acc[...] += lax.dot_general(
            left[...], right[...], (((1,), (1,)), ((), ())), preferred_element_type=F32
        )
        return carry

    lax.fori_loop(0, n // GROUP, gather_group, 0)

    def summed(f):
        top = (1 + 2 * f) * lines
        both = acc[top:top + lines, :] + acc[top + lines:top + 2 * lines, :]
        return both.reshape(planes, rows, cols)

    finish_edges(early_copies)
    perm = jnp.where(valid, extended(perm_ref[...], perm_row[...], 0, 0), 0.0)
    diag = 6.0 - K_SQUARED * perm
    shift = BETA * K_SQUARED * perm
    denom = diag * diag + shift * shift
    inv_real = diag / denom
    inv_imag = -shift / denom

    right_ref[0:planes] = rhs_ref[0:planes] - summed(3)
    right_ref[planes:] = rhs_ref[planes:] - summed(4)
    slope_ref[0:planes] = acc[0:lines, :].reshape(planes, rows, cols)
    for f in range(3):
        slope_ref[(1 + f) * planes:(2 + f) * planes] = summed(f)
    strips(1, right_ref[...])
    strips(2, slope_ref[0:2 * planes])
    strips(3, slope_ref[2 * planes:])
    late_copies = edge_copies(False)
    start_edges(late_copies)
    finish_edges(late_copies)

    def right_part(part):
        at = slice(part * planes, (part + 1) * planes)
        return jnp.where(valid, extended(right_ref[at], right_row[at], 1, part), 0.0)

    def slope(f):
        at = slice(f * planes, (f + 1) * planes)
        return extended(slope_ref[at], slope_row[at], 2 + f // 2, f % 2, corners=False)

    def precond(real, imag):
        return (
            OMEGA * (real * inv_real - imag * inv_imag),
            OMEGA * (real * inv_imag + imag * inv_real),
        )

    def swapped(v):
        return jnp.concatenate([v[planes:], v[:planes]], axis=0)

    def shifts(v):
        zero = jnp.zeros((1, *size[1:]), F32)
        z_next = jnp.concatenate([v[1:planes], zero, v[planes + 1:], zero], axis=0)
        z_last = jnp.concatenate([zero, v[:planes - 1], zero, v[planes:-1]], axis=0)
        x_next = pltpu.roll(v, rows - 1, 1)
        x_next = jnp.where(row_at == rows - 1, swapped(x_next), x_next)
        x_last = pltpu.roll(v, 1, 1)
        x_last = jnp.where(row_at == 0, swapped(x_last), x_last)
        return z_next, z_last, x_next, x_last, pltpu.roll(v, size[2] - 1, 2), pltpu.roll(v, 1, 2)

    def helm(v, around):
        z_next, z_last, x_next, x_last, y_next, y_last = around
        return diag * v - (z_next + z_last + x_next + x_last + y_next + y_last)

    def update(real, imag):
        z_real, z_imag = precond(real, imag)
        image_real = helm(z_real, shifts(z_real)) - shift * z_imag
        image_imag = helm(z_imag, shifts(z_imag)) + shift * z_real
        more_real, more_imag = precond(real - image_real, imag - image_imag)
        return z_real + more_real, z_imag + more_imag

    source = right_part(0), right_part(1)
    first = [jnp.where(inside, v, 0.0) for v in update(*source)]
    slopes = [slope(f) for f in range(4)]
    residual = []
    for v, origin in zip(first, source):
        around = shifts(v)
        z_next, z_last, x_next, x_last, y_next, y_last = around
        surface = slopes[0] * v + slopes[1] * (z_next - z_last)
        surface = surface + slopes[2] * (x_next - x_last) + slopes[3] * (y_next - y_last)
        residual.append(jnp.where(inside, origin - helm(v, around) - surface, 0.0))
    for part in range(2):
        res_ref[part * planes:(part + 1) * planes] = residual[part][:planes, :, :cols]
    res_write = pltpu.make_async_copy(res_ref, res_hbm, written.at[0])
    res_write.start()
    second = update(*residual)
    for part in range(2):
        both = first[part] + second[part]
        sol_ref[part * planes:(part + 1) * planes] = both[:planes, :, :cols]
    sol_write = pltpu.make_async_copy(sol_ref, sol_hbm, written.at[1])
    sol_write.start()
    for there, _, copy in early_copies + late_copies:
        pl.when(there)(copy.wait_send)

    def finish_block(k, carry):
        block_copy(k).wait_send()
        return carry

    lax.fori_loop(1, n, finish_block, 0)
    res_write.wait()
    sol_write.wait()


def write_out(sol_ref, res_ref, sol_out, res_out, sol_held, res_held, here, done):
    loads = (
        pltpu.make_async_copy(sol_ref, sol_held, here.at[0]),
        pltpu.make_async_copy(res_ref, res_held, here.at[1]),
    )
    stores = (
        pltpu.make_async_copy(sol_held, sol_out, done.at[0]),
        pltpu.make_async_copy(res_held, res_out, done.at[1]),
    )
    for load in loads:
        load.start()
    for load, store in zip(loads, stores):
        load.wait()
        store.start()
    for store in stores:
        store.wait()


def per_device(
    n_gx, n_gy,
    rhs_field, permittivity, surf_dist, surf_normal, surf_inc, surf_cell, surf_mask, surf_owner,
):
    planes, rows, cols = permittivity.shape
    points = surf_cell.shape[1]
    n = n_gx * n_gy
    lines = planes * rows
    field = jax.ShapeDtypeStruct((2 * planes, rows, cols), F32)
    hbm = pl.BlockSpec(memory_space=pltpu.HBM)
    owner = surf_owner.reshape(1, -1)
    operands = (
        rhs_field.reshape(field.shape), permittivity, surf_dist, surf_normal, surf_inc,
        surf_cell, surf_mask, owner,
    )
    deep = GROUP * CAP * points
    sol, res = pl.pallas_call(
        functools.partial(kernel, n_gx, n_gy),
        out_shape=(field, field),
        in_specs=[hbm] * 8,
        out_specs=(hbm, hbm),
        scratch_shapes=[
            *[pltpu.VMEM(x.shape, x.dtype) for x in operands],
            pltpu.VMEM((n, ROWS, points), F32),
            pltpu.VMEM((n, ROWS, points), F32),
            pltpu.VMEM((PARTS * lines, deep), BF16),
            pltpu.VMEM((cols, deep), BF16),
            pltpu.VMEM((PARTS * lines, cols), F32),
            pltpu.VMEM((2 * planes, rows, cols), F32),
            pltpu.VMEM((2 * planes, rows, cols), F32),
            pltpu.VMEM((4 * planes, rows, cols), F32),
            pltpu.VMEM((4 * planes, rows, cols), F32),
            pltpu.VMEM((planes, rows, cols), F32),
            pltpu.VMEM((2, 4, 8, 2 * lines), F32),
            pltpu.VMEM((2, 3, 4, 8, 2 * lines), F32),
            pltpu.VMEM(field.shape, F32),
            pltpu.VMEM(field.shape, F32),
            pltpu.SemaphoreType.DMA((8,)),
            pltpu.SemaphoreType.DMA((2,)),
            pltpu.SemaphoreType.DMA((n,)),
            pltpu.SemaphoreType.DMA((n,)),
            pltpu.SemaphoreType.DMA((2, 10)),
            pltpu.SemaphoreType.DMA((2, 10)),
        ],
        compiler_params=pltpu.CompilerParams(
            collective_id=0, has_side_effects=True, vmem_limit_bytes=64 * 1024 * 1024
        ),
    )(*operands)
    sol, res = pl.pallas_call(
        write_out,
        out_shape=(field, field),
        in_specs=[hbm] * 2,
        out_specs=(hbm, hbm),
        scratch_shapes=[
            pltpu.VMEM(field.shape, F32),
            pltpu.VMEM(field.shape, F32),
            pltpu.SemaphoreType.DMA((2,)),
            pltpu.SemaphoreType.DMA((2,)),
        ],
        compiler_params=pltpu.CompilerParams(vmem_limit_bytes=64 * 1024 * 1024),
    )(sol, res)
    return sol.reshape(rhs_field.shape), res.reshape(rhs_field.shape)


def solution(mesh):
    placed = (
        P(None, None, "gx", "gy"),
        P(None, "gx", "gy"),
        P(("gx", "gy"), None),
        P(None, ("gx", "gy"), None),
        P(None, ("gx", "gy"), None),
        P(("gx", "gy"), None),
        P(("gx", "gy"), None),
        P(("gx", "gy"), None),
    )
    return jax.shard_map(
        functools.partial(per_device, mesh.shape["gx"], mesh.shape["gy"]),
        mesh=mesh,
        in_specs=placed,
        out_specs=(P(None, None, "gx", "gy"), P(None, None, "gx", "gy")),
        check_vma=False,
    )
```

```python
import functools

import jax
import jax.numpy as jnp
from jax import lax
from jax.experimental import pallas as pl
from jax.experimental.pallas import tpu as pltpu
from jax.sharding import PartitionSpec as P

CAP = 2
K_SQUARED = 0.25
BETA = 0.5
OMEGA = 0.8
TAU = 1.0
FIELDS = 7
SENT = CAP * FIELDS
ROWS = -(-SENT // 8) * 8
PARTS = 11
GROUP = 8
REACH = 3
MESH = pl.DeviceIdType.MESH
F32 = jnp.float32
BF16 = jnp.bfloat16


def iota(shape, dim):
    return lax.broadcasted_iota(jnp.int32, shape, dim)


def kernel(
    n_gx, n_gy,
    rhs_hbm, perm_hbm, dist_hbm, normal_hbm, inc_hbm, cell_hbm, mask_hbm, owner_hbm,
    sol_hbm, res_hbm,
    rhs_ref, perm_ref, dist_ref, normal_ref, inc_ref, cell_ref, mask_ref, owner_ref,
    send, recv, left, right, acc, right_ref, right_row, slope_ref, slope_row, perm_row, strip_send, strip_recv,
    sol_ref, res_ref, loaded, written, block_out, block_in, halo_out, halo_in,
):
    gx, gy = lax.axis_index("gx"), lax.axis_index("gy")
    n = n_gx * n_gy
    me = gx * n_gy + gy
    blocks, points = cell_ref.shape
    planes, rows, cols = perm_ref.shape
    lines = planes * rows

    def peer(k):
        to = lax.rem(me + k, n)
        return to, (lax.div(to, n_gy), lax.rem(to, n_gy))

    barrier = pltpu.get_barrier_semaphore()

    def greet(k, carry):
        pl.semaphore_signal(barrier, inc=1, device_id=peer(k)[1], device_id_type=MESH)
        return carry

    lax.fori_loop(1, n, greet, 0)
    loads = [
        pltpu.make_async_copy(source, sink, loaded.at[i])
        for i, (source, sink) in enumerate((
            (owner_hbm, owner_ref), (cell_hbm, cell_ref), (mask_hbm, mask_ref),
            (dist_hbm, dist_ref), (normal_hbm, normal_ref), (inc_hbm, inc_ref),
            (perm_hbm, perm_ref), (rhs_hbm, rhs_ref),
        ))
    ]
    for load in loads:
        load.start()
    for load in loads[:6]:
        load.wait()

    weight = TAU * mask_ref[...].astype(F32)
    half = weight * dist_ref[...] * 0.5
    data = jnp.concatenate(
        [
            cell_ref[...].astype(F32), weight,
            half * normal_ref[0], half * normal_ref[1], half * normal_ref[2],
            weight * inc_ref[0], weight * inc_ref[1],
        ],
        axis=0,
    )
    wide = FIELDS * blocks
    lane_no = iota((blocks, wide), 1)
    lane_block = lane_no % blocks
    row_block = iota((blocks, wide), 0)
    square = (blocks, blocks)
    owner = jnp.where(iota(square, 0) == iota(square, 1), owner_ref[...].astype(F32), 0.0)
    owner = jnp.broadcast_to(jnp.sum(owner, axis=1, keepdims=True), (blocks, wide))
    owner_of = jnp.sum(jnp.where(row_block == lane_block, owner, 0.0), axis=0, keepdims=True)
    earlier = (owner == owner_of) & (row_block < lane_block)
    rank = jnp.sum(jnp.where(earlier, 1.0, 0.0), axis=0, keepdims=True)
    field_no = (iota((1, wide), 1) // blocks).astype(F32)
    target = owner_of * ROWS + rank * FIELDS + field_no
    slots = n * ROWS
    chosen = jnp.where(iota((slots, wide), 0).astype(F32) == target, 1.0, 0.0).astype(BF16)
    high = data.astype(BF16)
    rest = data - high.astype(F32)
    middle = rest.astype(BF16)
    low = (rest - middle.astype(F32)).astype(BF16)
    placed = jnp.dot(chosen, high, preferred_element_type=F32)
    placed = placed + jnp.dot(chosen, middle, preferred_element_type=F32)
    placed = placed + jnp.dot(chosen, low, preferred_element_type=F32)
    send[...] = placed.reshape(n, ROWS, points)

    pl.semaphore_wait(barrier, n - 1)

    def block_copy(k):
        to, where = peer(k)
        return pltpu.make_async_remote_copy(
            src_ref=send.at[to, pl.ds(0, SENT)], dst_ref=recv.at[k, pl.ds(0, SENT)],
            send_sem=block_out.at[k], recv_sem=block_in.at[k],
            device_id=where, device_id_type=MESH,
        )

    def start_block(k, carry):
        block_copy(k).start()
        return carry

    lax.fori_loop(1, n, start_block, 0)
    recv[0] = send[me]
    for load in loads[6:]:
        load.wait()

    def within(x, y):
        return (x >= 0) & (x < n_gx) & (y >= 0) & (y < n_gy)

    def strips(first, field):
        flat = field.reshape(2 * lines, cols)
        strip_send[0, first] = jnp.transpose(flat[:, cols - 128:])[120:128]
        strip_send[1, first] = jnp.transpose(flat[:, :128])[0:8]

    def edge_copies(early):
        moves = []
        for side, dx in enumerate((1, -1)):
            top = rows - REACH if dx == 1 else 0
            end = rows - 1 if dx == 1 else 0
            if early:
                moves.append((dx, 0, perm_ref.at[:, pl.ds(top, REACH)], perm_row.at[:, pl.ds(top, REACH)]))
            else:
                moves.append((dx, 0, right_ref.at[:, pl.ds(top, REACH)], right_row.at[:, pl.ds(top, REACH)]))
                moves.append((dx, 0, slope_ref.at[:, pl.ds(end, 1)], slope_row.at[:, pl.ds(end, 1)]))
        part = pl.ds(0, 1) if early else pl.ds(1, 3)
        for side, dy in enumerate((1, -1)):
            for dx in (-1, 0, 1):
                moves.append((dx, dy, strip_send.at[side, part], strip_recv.at[side, dx + 1, part]))
        out = []
        for number, (dx, dy, source, sink) in enumerate(moves):
            which = (0 if early else 1, number)
            out.append((
                within(gx + dx, gy + dy), within(gx - dx, gy - dy),
                pltpu.make_async_remote_copy(
                    src_ref=source, dst_ref=sink,
                    send_sem=halo_out.at[which], recv_sem=halo_in.at[which],
                    device_id=(gx + dx, gy + dy), device_id_type=MESH,
                ),
            ))
        return out

    def start_edges(copies):
        for there, _, copy in copies:
            pl.when(there)(copy.start)

    def finish_edges(copies):
        for there, comes, copy in copies:
            pl.when(comes)(copy.wait_recv)

    def beside_tile(dx, first):
        empty = jnp.zeros((112, 2 * lines), F32)
        stacked = jnp.concatenate(
            [strip_recv[1, dx + 1, first], empty, strip_recv[0, dx + 1, first]], axis=0
        )
        return jnp.transpose(stacked).reshape(2 * planes, rows, 128)

    size = (2 * planes, rows, cols + 128)
    row_at, col_at = iota(size, 1), iota(size, 2)
    other = iota(size, 0) >= planes
    row_own = jnp.where(other, jnp.where(row_at < 4, rows + row_at, row_at - rows), row_at)
    col_own = jnp.where(col_at < cols + 64, col_at, col_at - (cols + 128))
    row_all, col_all = gx * rows + row_own, gy * cols + col_own
    inside = (row_all >= 0) & (row_all < n_gx * rows) & (col_all >= 0) & (col_all < n_gy * cols)
    valid = inside & (row_own >= -REACH) & (row_own < rows + REACH)

    def extended(own, around, first, part, corners=True):
        at = slice(part * planes, (part + 1) * planes)
        side = beside_tile(0, first)[at]
        if corners:
            near = iota((planes, rows, 128), 1) < 4
            far = jnp.where(near, beside_tile(-1, first)[at], beside_tile(1, first)[at])
        else:
            far = jnp.zeros(side.shape, F32)
        return jnp.concatenate([
            jnp.concatenate([own, side], axis=2), jnp.concatenate([around, far], axis=2)
        ], axis=0)

    strips(0, jnp.concatenate([perm_ref[...], perm_ref[...]], axis=0))
    early_copies = edge_copies(True)
    start_edges(early_copies)

    acc[...] = jnp.zeros(acc.shape, F32)
    line_no = iota((lines, points), 0).astype(F32).astype(BF16)
    col_no = iota((cols, points), 0).astype(F32).astype(BF16)
    one, nil = jnp.ones((), BF16), jnp.zeros((), BF16)

    def spread(row, count):
        some = jnp.broadcast_to(row, (16, points)).astype(BF16)
        return jnp.concatenate([some] * (count // 16), axis=0)

    def gather_group(g, carry):
        for j in range(GROUP):
            k = g * GROUP + j

            @pl.when(k > 0)
            def _():
                block_copy(k).wait_recv()

        for j in range(GROUP):
            for r in range(CAP):
                tile = recv[g * GROUP + j, r * FIELDS:(r + 1) * FIELDS, :]
                at = slice((j * CAP + r) * points, (j * CAP + r + 1) * points)
                cell = tile[0:1]
                line = jnp.floor(cell * (1.0 / cols))
                column = cell - line * cols
                right[:, at] = jnp.where(col_no == spread(column, cols), one, nil)
                here = jnp.where(line_no == spread(line, lines), one, nil)
                left[0:lines, at] = here * spread(tile[1:2], lines)
                upper = tile.astype(BF16).astype(F32)
                lower = tile - upper
                for f in range(5):
                    for p, part in enumerate((upper, lower)):
                        top = (1 + 2 * f + p) * lines
                        left[top:top + lines, at] = here * spread(part[2 + f:3 + f], lines)
        acc[...] += lax.dot_general(
            left[...], right[...], (((1,), (1,)), ((), ())), preferred_element_type=F32
        )
        return carry

    lax.fori_loop(0, n // GROUP, gather_group, 0)

    def summed(f):
        top = (1 + 2 * f) * lines
        both = acc[top:top + lines, :] + acc[top + lines:top + 2 * lines, :]
        return both.reshape(planes, rows, cols)

    finish_edges(early_copies)
    perm = jnp.where(valid, extended(perm_ref[...], perm_row[...], 0, 0), 0.0)
    diag = 6.0 - K_SQUARED * perm
    shift = BETA * K_SQUARED * perm
    denom = diag * diag + shift * shift
    inv_real = diag / denom
    inv_imag = -shift / denom

    right_ref[0:planes] = rhs_ref[0:planes] - summed(3)
    right_ref[planes:] = rhs_ref[planes:] - summed(4)
    slope_ref[0:planes] = acc[0:lines, :].reshape(planes, rows, cols)
    for f in range(3):
        slope_ref[(1 + f) * planes:(2 + f) * planes] = summed(f)
    strips(1, right_ref[...])
    strips(2, slope_ref[0:2 * planes])
    strips(3, slope_ref[2 * planes:])
    late_copies = edge_copies(False)
    start_edges(late_copies)
    finish_edges(late_copies)

    def right_part(part):
        at = slice(part * planes, (part + 1) * planes)
        return jnp.where(valid, extended(right_ref[at], right_row[at], 1, part), 0.0)

    def slope(f):
        at = slice(f * planes, (f + 1) * planes)
        return extended(slope_ref[at], slope_row[at], 2 + f // 2, f % 2, corners=False)

    def precond(real, imag):
        return (
            OMEGA * (real * inv_real - imag * inv_imag),
            OMEGA * (real * inv_imag + imag * inv_real),
        )

    def swapped(v):
        return jnp.concatenate([v[planes:], v[:planes]], axis=0)

    def shifts(v):
        zero = jnp.zeros((1, *size[1:]), F32)
        z_next = jnp.concatenate([v[1:planes], zero, v[planes + 1:], zero], axis=0)
        z_last = jnp.concatenate([zero, v[:planes - 1], zero, v[planes:-1]], axis=0)
        x_next = pltpu.roll(v, rows - 1, 1)
        x_next = jnp.where(row_at == rows - 1, swapped(x_next), x_next)
        x_last = pltpu.roll(v, 1, 1)
        x_last = jnp.where(row_at == 0, swapped(x_last), x_last)
        return z_next, z_last, x_next, x_last, pltpu.roll(v, size[2] - 1, 2), pltpu.roll(v, 1, 2)

    def helm(v, around):
        z_next, z_last, x_next, x_last, y_next, y_last = around
        return diag * v - (z_next + z_last + x_next + x_last + y_next + y_last)

    def update(real, imag):
        z_real, z_imag = precond(real, imag)
        image_real = helm(z_real, shifts(z_real)) - shift * z_imag
        image_imag = helm(z_imag, shifts(z_imag)) + shift * z_real
        more_real, more_imag = precond(real - image_real, imag - image_imag)
        return z_real + more_real, z_imag + more_imag

    source = right_part(0), right_part(1)
    first = [jnp.where(inside, v, 0.0) for v in update(*source)]
    slopes = [slope(f) for f in range(4)]
    residual = []
    for v, origin in zip(first, source):
        around = shifts(v)
        z_next, z_last, x_next, x_last, y_next, y_last = around
        surface = slopes[0] * v + slopes[1] * (z_next - z_last)
        surface = surface + slopes[2] * (x_next - x_last) + slopes[3] * (y_next - y_last)
        residual.append(jnp.where(inside, origin - helm(v, around) - surface, 0.0))
    for part in range(2):
        res_ref[part * planes:(part + 1) * planes] = residual[part][:planes, :, :cols]
    res_write = pltpu.make_async_copy(res_ref, res_hbm, written.at[0])
    res_write.start()
    second = update(*residual)
    for part in range(2):
        both = first[part] + second[part]
        sol_ref[part * planes:(part + 1) * planes] = both[:planes, :, :cols]
    sol_write = pltpu.make_async_copy(sol_ref, sol_hbm, written.at[1])
    sol_write.start()
    for there, _, copy in early_copies + late_copies:
        pl.when(there)(copy.wait_send)

    def finish_block(k, carry):
        block_copy(k).wait_send()
        return carry

    lax.fori_loop(1, n, finish_block, 0)
    res_write.wait()
    sol_write.wait()


def write_out(sol_ref, res_ref, sol_out, res_out, sol_held, res_held, here, done):
    loads = (
        pltpu.make_async_copy(sol_ref, sol_held, here.at[0]),
        pltpu.make_async_copy(res_ref, res_held, here.at[1]),
    )
    stores = (
        pltpu.make_async_copy(sol_held, sol_out, done.at[0]),
        pltpu.make_async_copy(res_held, res_out, done.at[1]),
    )
    for load in loads:
        load.start()
    for load, store in zip(loads, stores):
        load.wait()
        store.start()
    for store in stores:
        store.wait()


def per_device(
    n_gx, n_gy,
    rhs_field, permittivity, surf_dist, surf_normal, surf_inc, surf_cell, surf_mask, surf_owner,
):
    planes, rows, cols = permittivity.shape
    points = surf_cell.shape[1]
    n = n_gx * n_gy
    lines = planes * rows
    field = jax.ShapeDtypeStruct((2 * planes, rows, cols), F32)
    hbm = pl.BlockSpec(memory_space=pltpu.HBM)
    owner = surf_owner.reshape(1, -1)
    operands = (
        rhs_field.reshape(field.shape), permittivity, surf_dist, surf_normal, surf_inc,
        surf_cell, surf_mask, owner,
    )
    deep = GROUP * CAP * points
    sol, res = pl.pallas_call(
        functools.partial(kernel, n_gx, n_gy),
        out_shape=(field, field),
        in_specs=[hbm] * 8,
        out_specs=(hbm, hbm),
        scratch_shapes=[
            *[pltpu.VMEM(x.shape, x.dtype) for x in operands],
            pltpu.VMEM((n, ROWS, points), F32),
            pltpu.VMEM((n, ROWS, points), F32),
            pltpu.VMEM((PARTS * lines, deep), BF16),
            pltpu.VMEM((cols, deep), BF16),
            pltpu.VMEM((PARTS * lines, cols), F32),
            pltpu.VMEM((2 * planes, rows, cols), F32),
            pltpu.VMEM((2 * planes, rows, cols), F32),
            pltpu.VMEM((4 * planes, rows, cols), F32),
            pltpu.VMEM((4 * planes, rows, cols), F32),
            pltpu.VMEM((planes, rows, cols), F32),
            pltpu.VMEM((2, 4, 8, 2 * lines), F32),
            pltpu.VMEM((2, 3, 4, 8, 2 * lines), F32),
            pltpu.VMEM(field.shape, F32),
            pltpu.VMEM(field.shape, F32),
            pltpu.SemaphoreType.DMA((8,)),
            pltpu.SemaphoreType.DMA((2,)),
            pltpu.SemaphoreType.DMA((n,)),
            pltpu.SemaphoreType.DMA((n,)),
            pltpu.SemaphoreType.DMA((2, 10)),
            pltpu.SemaphoreType.DMA((2, 10)),
        ],
        compiler_params=pltpu.CompilerParams(
            collective_id=0, has_side_effects=True, vmem_limit_bytes=64 * 1024 * 1024
        ),
    )(*operands)
    sol, res = pl.pallas_call(
        write_out,
        out_shape=(field, field),
        in_specs=[hbm] * 2,
        out_specs=(hbm, hbm),
        scratch_shapes=[
            pltpu.VMEM(field.shape, F32),
            pltpu.VMEM(field.shape, F32),
            pltpu.SemaphoreType.DMA((2,)),
            pltpu.SemaphoreType.DMA((2,)),
        ],
        compiler_params=pltpu.CompilerParams(vmem_limit_bytes=64 * 1024 * 1024),
    )(sol, res)
    return sol.reshape(rhs_field.shape), res.reshape(rhs_field.shape)


def solution(mesh):
    placed = (
        P(None, None, "gx", "gy"),
        P(None, "gx", "gy"),
        P(("gx", "gy"), None),
        P(None, ("gx", "gy"), None),
        P(None, ("gx", "gy"), None),
        P(("gx", "gy"), None),
        P(("gx", "gy"), None),
        P(("gx", "gy"), None),
    )
    return jax.shard_map(
        functools.partial(per_device, mesh.shape["gx"], mesh.shape["gy"]),
        mesh=mesh,
        in_specs=placed,
        out_specs=(P(None, None, "gx", "gy"), P(None, None, "gx", "gy")),
        check_vma=False,
    )
```

```python
import functools

import jax
import jax.numpy as jnp
from jax import lax
from jax.experimental import pallas as pl
from jax.experimental.pallas import tpu as pltpu
from jax.sharding import PartitionSpec as P

CAP = 2
K_SQUARED = 0.25
BETA = 0.5
OMEGA = 0.8
TAU = 1.0
FIELDS = 7
SENT = CAP * FIELDS
ROWS = -(-SENT // 8) * 8
PARTS = 11
GROUP = 8
REACH = 3
MESH = pl.DeviceIdType.MESH
F32 = jnp.float32
BF16 = jnp.bfloat16


def iota(shape, dim):
    return lax.broadcasted_iota(jnp.int32, shape, dim)


def kernel(
    n_gx, n_gy,
    rhs_hbm, perm_hbm, dist_hbm, normal_hbm, inc_hbm, cell_hbm, mask_hbm, owner_hbm,
    sol_hbm, res_hbm,
    rhs_ref, perm_ref, dist_ref, normal_ref, inc_ref, cell_ref, mask_ref, owner_ref,
    send, recv, left, right, acc, right_ref, right_row, slope_ref, slope_row, perm_row, strip_send, strip_recv,
    sol_ref, res_ref, loaded, written, block_out, block_in, halo_out, halo_in,
):
    gx, gy = lax.axis_index("gx"), lax.axis_index("gy")
    n = n_gx * n_gy
    me = gx * n_gy + gy
    blocks, points = cell_ref.shape
    planes, rows, cols = perm_ref.shape
    lines = planes * rows

    def peer(k):
        to = lax.rem(me + k, n)
        return to, (lax.div(to, n_gy), lax.rem(to, n_gy))

    barrier = pltpu.get_barrier_semaphore()

    def greet(k, carry):
        pl.semaphore_signal(barrier, inc=1, device_id=peer(k)[1], device_id_type=MESH)
        return carry

    lax.fori_loop(1, n, greet, 0)
    loads = [
        pltpu.make_async_copy(source, sink, loaded.at[i])
        for i, (source, sink) in enumerate((
            (owner_hbm, owner_ref), (cell_hbm, cell_ref), (mask_hbm, mask_ref),
            (dist_hbm, dist_ref), (normal_hbm, normal_ref), (inc_hbm, inc_ref),
            (perm_hbm, perm_ref), (rhs_hbm, rhs_ref),
        ))
    ]
    for load in loads:
        load.start()
    for load in loads[:6]:
        load.wait()

    weight = TAU * mask_ref[...].astype(F32)
    half = weight * dist_ref[...] * 0.5
    data = jnp.concatenate(
        [
            cell_ref[...].astype(F32), weight,
            half * normal_ref[0], half * normal_ref[1], half * normal_ref[2],
            weight * inc_ref[0], weight * inc_ref[1],
        ],
        axis=0,
    )
    wide = FIELDS * blocks
    lane_no = iota((blocks, wide), 1)
    lane_block = lane_no % blocks
    row_block = iota((blocks, wide), 0)
    square = (blocks, blocks)
    owner = jnp.where(iota(square, 0) == iota(square, 1), owner_ref[...].astype(F32), 0.0)
    owner = jnp.broadcast_to(jnp.sum(owner, axis=1, keepdims=True), (blocks, wide))
    owner_of = jnp.sum(jnp.where(row_block == lane_block, owner, 0.0), axis=0, keepdims=True)
    earlier = (owner == owner_of) & (row_block < lane_block)
    rank = jnp.sum(jnp.where(earlier, 1.0, 0.0), axis=0, keepdims=True)
    field_no = (iota((1, wide), 1) // blocks).astype(F32)
    target = owner_of * ROWS + rank * FIELDS + field_no
    slots = n * ROWS
    chosen = jnp.where(iota((slots, wide), 0).astype(F32) == target, 1.0, 0.0).astype(BF16)
    high = data.astype(BF16)
    rest = data - high.astype(F32)
    middle = rest.astype(BF16)
    low = (rest - middle.astype(F32)).astype(BF16)
    placed = jnp.dot(chosen, high, preferred_element_type=F32)
    placed = placed + jnp.dot(chosen, middle, preferred_element_type=F32)
    placed = placed + jnp.dot(chosen, low, preferred_element_type=F32)
    send[...] = placed.reshape(n, ROWS, points)

    pl.semaphore_wait(barrier, n - 1)

    def block_copy(k):
        to, where = peer(k)
        return pltpu.make_async_remote_copy(
            src_ref=send.at[to, pl.ds(0, SENT)], dst_ref=recv.at[k, pl.ds(0, SENT)],
            send_sem=block_out.at[k], recv_sem=block_in.at[k],
            device_id=where, device_id_type=MESH,
        )

    def start_block(k, carry):
        block_copy(k).start()
        return carry

    lax.fori_loop(1, n, start_block, 0)
    recv[0] = send[me]
    for load in loads[6:]:
        load.wait()

    def within(x, y):
        return (x >= 0) & (x < n_gx) & (y >= 0) & (y < n_gy)

    def strips(first, field):
        flat = field.reshape(2 * lines, cols)
        strip_send[0, first] = jnp.transpose(flat[:, cols - 128:])[120:128]
        strip_send[1, first] = jnp.transpose(flat[:, :128])[0:8]

    def edge_copies(early):
        moves = []
        for side, dx in enumerate((1, -1)):
            top = rows - REACH if dx == 1 else 0
            end = rows - 1 if dx == 1 else 0
            if early:
                moves.append((dx, 0, perm_ref.at[:, pl.ds(top, REACH)], perm_row.at[:, pl.ds(top, REACH)]))
            else:
                moves.append((dx, 0, right_ref.at[:, pl.ds(top, REACH)], right_row.at[:, pl.ds(top, REACH)]))
                moves.append((dx, 0, slope_ref.at[:, pl.ds(end, 1)], slope_row.at[:, pl.ds(end, 1)]))
        part = pl.ds(0, 1) if early else pl.ds(1, 3)
        for side, dy in enumerate((1, -1)):
            for dx in (-1, 0, 1):
                moves.append((dx, dy, strip_send.at[side, part], strip_recv.at[side, dx + 1, part]))
        out = []
        for number, (dx, dy, source, sink) in enumerate(moves):
            which = (0 if early else 1, number)
            out.append((
                within(gx + dx, gy + dy), within(gx - dx, gy - dy),
                pltpu.make_async_remote_copy(
                    src_ref=source, dst_ref=sink,
                    send_sem=halo_out.at[which], recv_sem=halo_in.at[which],
                    device_id=(gx + dx, gy + dy), device_id_type=MESH,
                ),
            ))
        return out

    def start_edges(copies):
        for there, _, copy in copies:
            pl.when(there)(copy.start)

    def finish_edges(copies):
        for there, comes, copy in copies:
            pl.when(comes)(copy.wait_recv)

    def beside_tile(dx, first):
        empty = jnp.zeros((112, 2 * lines), F32)
        stacked = jnp.concatenate(
            [strip_recv[1, dx + 1, first], empty, strip_recv[0, dx + 1, first]], axis=0
        )
        return jnp.transpose(stacked).reshape(2 * planes, rows, 128)

    size = (2 * planes, rows, cols + 128)
    row_at, col_at = iota(size, 1), iota(size, 2)
    other = iota(size, 0) >= planes
    row_own = jnp.where(other, jnp.where(row_at < 4, rows + row_at, row_at - rows), row_at)
    col_own = jnp.where(col_at < cols + 64, col_at, col_at - (cols + 128))
    row_all, col_all = gx * rows + row_own, gy * cols + col_own
    inside = (row_all >= 0) & (row_all < n_gx * rows) & (col_all >= 0) & (col_all < n_gy * cols)
    valid = inside & (row_own >= -REACH) & (row_own < rows + REACH)

    def extended(own, around, first, part, corners=True):
        at = slice(part * planes, (part + 1) * planes)
        side = beside_tile(0, first)[at]
        if corners:
            near = iota((planes, rows, 128), 1) < 4
            far = jnp.where(near, beside_tile(-1, first)[at], beside_tile(1, first)[at])
        else:
            far = jnp.zeros(side.shape, F32)
        return jnp.concatenate([
            jnp.concatenate([own, side], axis=2), jnp.concatenate([around, far], axis=2)
        ], axis=0)

    strips(0, jnp.concatenate([perm_ref[...], perm_ref[...]], axis=0))
    early_copies = edge_copies(True)
    start_edges(early_copies)

    acc[...] = jnp.zeros(acc.shape, F32)
    line_no = iota((lines, points), 0).astype(F32).astype(BF16)
    col_no = iota((cols, points), 0).astype(F32).astype(BF16)
    one, nil = jnp.ones((), BF16), jnp.zeros((), BF16)

    def spread(row, count):
        some = jnp.broadcast_to(row, (16, points)).astype(BF16)
        return jnp.concatenate([some] * (count // 16), axis=0)

    def gather_group(g, carry):
        for j in range(GROUP):
            k = g * GROUP + j

            @pl.when(k > 0)
            def _():
                block_copy(k).wait_recv()

        for j in range(GROUP):
            for r in range(CAP):
                tile = recv[g * GROUP + j, r * FIELDS:(r + 1) * FIELDS, :]
                at = slice((j * CAP + r) * points, (j * CAP + r + 1) * points)
                cell = tile[0:1]
                line = jnp.floor(cell * (1.0 / cols))
                column = cell - line * cols
                right[:, at] = jnp.where(col_no == spread(column, cols), one, nil)
                here = jnp.where(line_no == spread(line, lines), one, nil)
                left[0:lines, at] = here * spread(tile[1:2], lines)
                upper = tile.astype(BF16).astype(F32)
                lower = tile - upper
                for f in range(5):
                    for p, part in enumerate((upper, lower)):
                        top = (1 + 2 * f + p) * lines
                        left[top:top + lines, at] = here * spread(part[2 + f:3 + f], lines)
        acc[...] += lax.dot_general(
            left[...], right[...], (((1,), (1,)), ((), ())), preferred_element_type=F32
        )
        return carry

    groups = n // GROUP
    lax.fori_loop(0, groups - 1, gather_group, 0)
    finish_edges(early_copies)
    perm = jnp.where(valid, extended(perm_ref[...], perm_row[...], 0, 0), 0.0)
    diag = 6.0 - K_SQUARED * perm
    shift = BETA * K_SQUARED * perm
    denom = diag * diag + shift * shift
    inv_real = diag / denom
    inv_imag = -shift / denom
    gather_group(groups - 1, 0)

    def summed(f):
        top = (1 + 2 * f) * lines
        both = acc[top:top + lines, :] + acc[top + lines:top + 2 * lines, :]
        return both.reshape(planes, rows, cols)

    right_ref[0:planes] = rhs_ref[0:planes] - summed(3)
    right_ref[planes:] = rhs_ref[planes:] - summed(4)
    slope_ref[0:planes] = acc[0:lines, :].reshape(planes, rows, cols)
    for f in range(3):
        slope_ref[(1 + f) * planes:(2 + f) * planes] = summed(f)
    strips(1, right_ref[...])
    strips(2, slope_ref[0:2 * planes])
    strips(3, slope_ref[2 * planes:])
    late_copies = edge_copies(False)
    start_edges(late_copies)
    finish_edges(late_copies)

    def right_part(part):
        at = slice(part * planes, (part + 1) * planes)
        return jnp.where(valid, extended(right_ref[at], right_row[at], 1, part), 0.0)

    def slope(f):
        at = slice(f * planes, (f + 1) * planes)
        return extended(slope_ref[at], slope_row[at], 2 + f // 2, f % 2, corners=False)

    def precond(real, imag):
        return (
            OMEGA * (real * inv_real - imag * inv_imag),
            OMEGA * (real * inv_imag + imag * inv_real),
        )

    def swapped(v):
        return jnp.concatenate([v[planes:], v[:planes]], axis=0)

    def shifts(v):
        zero = jnp.zeros((1, *size[1:]), F32)
        z_next = jnp.concatenate([v[1:planes], zero, v[planes + 1:], zero], axis=0)
        z_last = jnp.concatenate([zero, v[:planes - 1], zero, v[planes:-1]], axis=0)
        x_next = pltpu.roll(v, rows - 1, 1)
        x_next = jnp.where(row_at == rows - 1, swapped(x_next), x_next)
        x_last = pltpu.roll(v, 1, 1)
        x_last = jnp.where(row_at == 0, swapped(x_last), x_last)
        return z_next, z_last, x_next, x_last, pltpu.roll(v, size[2] - 1, 2), pltpu.roll(v, 1, 2)

    def helm(v, around):
        z_next, z_last, x_next, x_last, y_next, y_last = around
        return diag * v - (z_next + z_last + x_next + x_last + y_next + y_last)

    def update(real, imag):
        z_real, z_imag = precond(real, imag)
        image_real = helm(z_real, shifts(z_real)) - shift * z_imag
        image_imag = helm(z_imag, shifts(z_imag)) + shift * z_real
        more_real, more_imag = precond(real - image_real, imag - image_imag)
        return z_real + more_real, z_imag + more_imag

    source = right_part(0), right_part(1)
    first = [jnp.where(inside, v, 0.0) for v in update(*source)]
    slopes = [slope(f) for f in range(4)]
    residual = []
    for v, origin in zip(first, source):
        around = shifts(v)
        z_next, z_last, x_next, x_last, y_next, y_last = around
        surface = slopes[0] * v + slopes[1] * (z_next - z_last)
        surface = surface + slopes[2] * (x_next - x_last) + slopes[3] * (y_next - y_last)
        residual.append(jnp.where(inside, origin - helm(v, around) - surface, 0.0))
    for part in range(2):
        res_ref[part * planes:(part + 1) * planes] = residual[part][:planes, :, :cols]
    res_write = pltpu.make_async_copy(res_ref, res_hbm, written.at[0])
    res_write.start()
    second = update(*residual)
    for part in range(2):
        both = first[part] + second[part]
        sol_ref[part * planes:(part + 1) * planes] = both[:planes, :, :cols]
    sol_write = pltpu.make_async_copy(sol_ref, sol_hbm, written.at[1])
    sol_write.start()
    for there, _, copy in early_copies + late_copies:
        pl.when(there)(copy.wait_send)

    def finish_block(k, carry):
        block_copy(k).wait_send()
        return carry

    lax.fori_loop(1, n, finish_block, 0)
    res_write.wait()
    sol_write.wait()


def write_out(sol_ref, res_ref, sol_out, res_out, sol_held, res_held, here, done):
    loads = (
        pltpu.make_async_copy(sol_ref, sol_held, here.at[0]),
        pltpu.make_async_copy(res_ref, res_held, here.at[1]),
    )
    stores = (
        pltpu.make_async_copy(sol_held, sol_out, done.at[0]),
        pltpu.make_async_copy(res_held, res_out, done.at[1]),
    )
    for load in loads:
        load.start()
    for load, store in zip(loads, stores):
        load.wait()
        store.start()
    for store in stores:
        store.wait()


def per_device(
    n_gx, n_gy,
    rhs_field, permittivity, surf_dist, surf_normal, surf_inc, surf_cell, surf_mask, surf_owner,
):
    planes, rows, cols = permittivity.shape
    points = surf_cell.shape[1]
    n = n_gx * n_gy
    lines = planes * rows
    field = jax.ShapeDtypeStruct((2 * planes, rows, cols), F32)
    hbm = pl.BlockSpec(memory_space=pltpu.HBM)
    owner = surf_owner.reshape(1, -1)
    operands = (
        rhs_field.reshape(field.shape), permittivity, surf_dist, surf_normal, surf_inc,
        surf_cell, surf_mask, owner,
    )
    deep = GROUP * CAP * points
    sol, res = pl.pallas_call(
        functools.partial(kernel, n_gx, n_gy),
        out_shape=(field, field),
        in_specs=[hbm] * 8,
        out_specs=(hbm, hbm),
        scratch_shapes=[
            *[pltpu.VMEM(x.shape, x.dtype) for x in operands],
            pltpu.VMEM((n, ROWS, points), F32),
            pltpu.VMEM((n, ROWS, points), F32),
            pltpu.VMEM((PARTS * lines, deep), BF16),
            pltpu.VMEM((cols, deep), BF16),
            pltpu.VMEM((PARTS * lines, cols), F32),
            pltpu.VMEM((2 * planes, rows, cols), F32),
            pltpu.VMEM((2 * planes, rows, cols), F32),
            pltpu.VMEM((4 * planes, rows, cols), F32),
            pltpu.VMEM((4 * planes, rows, cols), F32),
            pltpu.VMEM((planes, rows, cols), F32),
            pltpu.VMEM((2, 4, 8, 2 * lines), F32),
            pltpu.VMEM((2, 3, 4, 8, 2 * lines), F32),
            pltpu.VMEM(field.shape, F32),
            pltpu.VMEM(field.shape, F32),
            pltpu.SemaphoreType.DMA((8,)),
            pltpu.SemaphoreType.DMA((2,)),
            pltpu.SemaphoreType.DMA((n,)),
            pltpu.SemaphoreType.DMA((n,)),
            pltpu.SemaphoreType.DMA((2, 10)),
            pltpu.SemaphoreType.DMA((2, 10)),
        ],
        compiler_params=pltpu.CompilerParams(
            collective_id=0, has_side_effects=True, vmem_limit_bytes=64 * 1024 * 1024
        ),
    )(*operands)
    sol, res = pl.pallas_call(
        write_out,
        out_shape=(field, field),
        in_specs=[hbm] * 2,
        out_specs=(hbm, hbm),
        scratch_shapes=[
            pltpu.VMEM(field.shape, F32),
            pltpu.VMEM(field.shape, F32),
            pltpu.SemaphoreType.DMA((2,)),
            pltpu.SemaphoreType.DMA((2,)),
        ],
        compiler_params=pltpu.CompilerParams(vmem_limit_bytes=64 * 1024 * 1024),
    )(sol, res)
    return sol.reshape(rhs_field.shape), res.reshape(rhs_field.shape)


def solution(mesh):
    placed = (
        P(None, None, "gx", "gy"),
        P(None, "gx", "gy"),
        P(("gx", "gy"), None),
        P(None, ("gx", "gy"), None),
        P(None, ("gx", "gy"), None),
        P(("gx", "gy"), None),
        P(("gx", "gy"), None),
        P(("gx", "gy"), None),
    )
    return jax.shard_map(
        functools.partial(per_device, mesh.shape["gx"], mesh.shape["gy"]),
        mesh=mesh,
        in_specs=placed,
        out_specs=(P(None, None, "gx", "gy"), P(None, None, "gx", "gy")),
        check_vma=False,
    )
```

```python
import functools

import jax
import jax.numpy as jnp
from jax import lax
from jax.experimental import pallas as pl
from jax.experimental.pallas import tpu as pltpu
from jax.sharding import PartitionSpec as P

CAP = 2
K_SQUARED = 0.25
BETA = 0.5
OMEGA = 0.8
TAU = 1.0
FIELDS = 7
SENT = CAP * FIELDS
ROWS = -(-SENT // 8) * 8
PARTS = 11
GROUP = 4
REACH = 3
MESH = pl.DeviceIdType.MESH
F32 = jnp.float32
BF16 = jnp.bfloat16


def iota(shape, dim):
    return lax.broadcasted_iota(jnp.int32, shape, dim)


def kernel(
    n_gx, n_gy,
    rhs_hbm, perm_hbm, dist_hbm, normal_hbm, inc_hbm, cell_hbm, mask_hbm, owner_hbm,
    sol_hbm, res_hbm,
    rhs_ref, perm_ref, dist_ref, normal_ref, inc_ref, cell_ref, mask_ref, owner_ref,
    send, recv, left, right, acc, right_ref, right_row, slope_ref, slope_row, perm_row, strip_send, strip_recv,
    sol_ref, res_ref, loaded, written, block_out, block_in, halo_out, halo_in,
):
    gx, gy = lax.axis_index("gx"), lax.axis_index("gy")
    n = n_gx * n_gy
    me = gx * n_gy + gy
    blocks, points = cell_ref.shape
    planes, rows, cols = perm_ref.shape
    lines = planes * rows

    def peer(k):
        to = lax.rem(me + k, n)
        return to, (lax.div(to, n_gy), lax.rem(to, n_gy))

    barrier = pltpu.get_barrier_semaphore()

    def greet(k, carry):
        pl.semaphore_signal(barrier, inc=1, device_id=peer(k)[1], device_id_type=MESH)
        return carry

    lax.fori_loop(1, n, greet, 0)
    loads = [
        pltpu.make_async_copy(source, sink, loaded.at[i])
        for i, (source, sink) in enumerate((
            (owner_hbm, owner_ref), (cell_hbm, cell_ref), (mask_hbm, mask_ref),
            (dist_hbm, dist_ref), (normal_hbm, normal_ref), (inc_hbm, inc_ref),
            (perm_hbm, perm_ref), (rhs_hbm, rhs_ref),
        ))
    ]
    for load in loads:
        load.start()
    for load in loads[:6]:
        load.wait()

    weight = TAU * mask_ref[...].astype(F32)
    half = weight * dist_ref[...] * 0.5
    data = jnp.concatenate(
        [
            cell_ref[...].astype(F32), weight,
            half * normal_ref[0], half * normal_ref[1], half * normal_ref[2],
            weight * inc_ref[0], weight * inc_ref[1],
        ],
        axis=0,
    )
    wide = FIELDS * blocks
    lane_no = iota((blocks, wide), 1)
    lane_block = lane_no % blocks
    row_block = iota((blocks, wide), 0)
    square = (blocks, blocks)
    owner = jnp.where(iota(square, 0) == iota(square, 1), owner_ref[...].astype(F32), 0.0)
    owner = jnp.broadcast_to(jnp.sum(owner, axis=1, keepdims=True), (blocks, wide))
    owner_of = jnp.sum(jnp.where(row_block == lane_block, owner, 0.0), axis=0, keepdims=True)
    earlier = (owner == owner_of) & (row_block < lane_block)
    rank = jnp.sum(jnp.where(earlier, 1.0, 0.0), axis=0, keepdims=True)
    field_no = (iota((1, wide), 1) // blocks).astype(F32)
    target = owner_of * ROWS + rank * FIELDS + field_no
    slots = n * ROWS
    chosen = jnp.where(iota((slots, wide), 0).astype(F32) == target, 1.0, 0.0).astype(BF16)
    high = data.astype(BF16)
    rest = data - high.astype(F32)
    middle = rest.astype(BF16)
    low = (rest - middle.astype(F32)).astype(BF16)
    placed = jnp.dot(chosen, high, preferred_element_type=F32)
    placed = placed + jnp.dot(chosen, middle, preferred_element_type=F32)
    placed = placed + jnp.dot(chosen, low, preferred_element_type=F32)
    send[...] = placed.reshape(n, ROWS, points)

    pl.semaphore_wait(barrier, n - 1)

    def block_copy(k):
        to, where = peer(k)
        return pltpu.make_async_remote_copy(
            src_ref=send.at[to, pl.ds(0, SENT)], dst_ref=recv.at[k, pl.ds(0, SENT)],
            send_sem=block_out.at[k], recv_sem=block_in.at[k],
            device_id=where, device_id_type=MESH,
        )

    def start_block(k, carry):
        block_copy(k).start()
        return carry

    lax.fori_loop(1, n, start_block, 0)
    recv[0] = send[me]
    for load in loads[6:]:
        load.wait()

    def within(x, y):
        return (x >= 0) & (x < n_gx) & (y >= 0) & (y < n_gy)

    def strips(first, field):
        flat = field.reshape(2 * lines, cols)
        strip_send[0, first] = jnp.transpose(flat[:, cols - 128:])[120:128]
        strip_send[1, first] = jnp.transpose(flat[:, :128])[0:8]

    def edge_copies(early):
        moves = []
        for side, dx in enumerate((1, -1)):
            top = rows - REACH if dx == 1 else 0
            end = rows - 1 if dx == 1 else 0
            if early:
                moves.append((dx, 0, perm_ref.at[:, pl.ds(top, REACH)], perm_row.at[:, pl.ds(top, REACH)]))
            else:
                moves.append((dx, 0, right_ref.at[:, pl.ds(top, REACH)], right_row.at[:, pl.ds(top, REACH)]))
                moves.append((dx, 0, slope_ref.at[:, pl.ds(end, 1)], slope_row.at[:, pl.ds(end, 1)]))
        part = pl.ds(0, 1) if early else pl.ds(1, 3)
        for side, dy in enumerate((1, -1)):
            for dx in (-1, 0, 1):
                moves.append((dx, dy, strip_send.at[side, part], strip_recv.at[side, dx + 1, part]))
        out = []
        for number, (dx, dy, source, sink) in enumerate(moves):
            which = (0 if early else 1, number)
            out.append((
                within(gx + dx, gy + dy), within(gx - dx, gy - dy),
                pltpu.make_async_remote_copy(
                    src_ref=source, dst_ref=sink,
                    send_sem=halo_out.at[which], recv_sem=halo_in.at[which],
                    device_id=(gx + dx, gy + dy), device_id_type=MESH,
                ),
            ))
        return out

    def start_edges(copies):
        for there, _, copy in copies:
            pl.when(there)(copy.start)

    def finish_edges(copies):
        for there, comes, copy in copies:
            pl.when(comes)(copy.wait_recv)

    def beside_tile(dx, first):
        empty = jnp.zeros((112, 2 * lines), F32)
        stacked = jnp.concatenate(
            [strip_recv[1, dx + 1, first], empty, strip_recv[0, dx + 1, first]], axis=0
        )
        return jnp.transpose(stacked).reshape(2 * planes, rows, 128)

    size = (2 * planes, rows, cols + 128)
    row_at, col_at = iota(size, 1), iota(size, 2)
    other = iota(size, 0) >= planes
    row_own = jnp.where(other, jnp.where(row_at < 4, rows + row_at, row_at - rows), row_at)
    col_own = jnp.where(col_at < cols + 64, col_at, col_at - (cols + 128))
    row_all, col_all = gx * rows + row_own, gy * cols + col_own
    inside = (row_all >= 0) & (row_all < n_gx * rows) & (col_all >= 0) & (col_all < n_gy * cols)
    valid = inside & (row_own >= -REACH) & (row_own < rows + REACH)

    def extended(own, around, first, part, corners=True):
        at = slice(part * planes, (part + 1) * planes)
        side = beside_tile(0, first)[at]
        if corners:
            near = iota((planes, rows, 128), 1) < 4
            far = jnp.where(near, beside_tile(-1, first)[at], beside_tile(1, first)[at])
        else:
            far = jnp.zeros(side.shape, F32)
        return jnp.concatenate([
            jnp.concatenate([own, side], axis=2), jnp.concatenate([around, far], axis=2)
        ], axis=0)

    strips(0, jnp.concatenate([perm_ref[...], perm_ref[...]], axis=0))
    early_copies = edge_copies(True)
    start_edges(early_copies)

    acc[...] = jnp.zeros(acc.shape, F32)
    line_no = iota((lines, points), 0).astype(F32).astype(BF16)
    col_no = iota((cols, points), 0).astype(F32).astype(BF16)
    one, nil = jnp.ones((), BF16), jnp.zeros((), BF16)

    def spread(row, count):
        some = jnp.broadcast_to(row, (16, points)).astype(BF16)
        return jnp.concatenate([some] * (count // 16), axis=0)

    def gather_group(g, carry):
        for j in range(GROUP):
            k = g * GROUP + j

            @pl.when(k > 0)
            def _():
                block_copy(k).wait_recv()

        for j in range(GROUP):
            for r in range(CAP):
                tile = recv[g * GROUP + j, r * FIELDS:(r + 1) * FIELDS, :]
                at = slice((j * CAP + r) * points, (j * CAP + r + 1) * points)
                cell = tile[0:1]
                line = jnp.floor(cell * (1.0 / cols))
                column = cell - line * cols
                right[:, at] = jnp.where(col_no == spread(column, cols), one, nil)
                here = jnp.where(line_no == spread(line, lines), one, nil)
                left[0:lines, at] = here * spread(tile[1:2], lines)
                upper = tile.astype(BF16).astype(F32)
                lower = tile - upper
                for f in range(5):
                    for p, part in enumerate((upper, lower)):
                        top = (1 + 2 * f + p) * lines
                        left[top:top + lines, at] = here * spread(part[2 + f:3 + f], lines)
        acc[...] += lax.dot_general(
            left[...], right[...], (((1,), (1,)), ((), ())), preferred_element_type=F32
        )
        return carry

    lax.fori_loop(0, n // GROUP, gather_group, 0)

    def summed(f):
        top = (1 + 2 * f) * lines
        both = acc[top:top + lines, :] + acc[top + lines:top + 2 * lines, :]
        return both.reshape(planes, rows, cols)

    finish_edges(early_copies)
    perm = jnp.where(valid, extended(perm_ref[...], perm_row[...], 0, 0), 0.0)
    diag = 6.0 - K_SQUARED * perm
    shift = BETA * K_SQUARED * perm
    denom = diag * diag + shift * shift
    inv_real = diag / denom
    inv_imag = -shift / denom

    right_ref[0:planes] = rhs_ref[0:planes] - summed(3)
    right_ref[planes:] = rhs_ref[planes:] - summed(4)
    slope_ref[0:planes] = acc[0:lines, :].reshape(planes, rows, cols)
    for f in range(3):
        slope_ref[(1 + f) * planes:(2 + f) * planes] = summed(f)
    strips(1, right_ref[...])
    strips(2, slope_ref[0:2 * planes])
    strips(3, slope_ref[2 * planes:])
    late_copies = edge_copies(False)
    start_edges(late_copies)
    finish_edges(late_copies)

    def right_part(part):
        at = slice(part * planes, (part + 1) * planes)
        return jnp.where(valid, extended(right_ref[at], right_row[at], 1, part), 0.0)

    def slope(f):
        at = slice(f * planes, (f + 1) * planes)
        return extended(slope_ref[at], slope_row[at], 2 + f // 2, f % 2, corners=False)

    def precond(real, imag):
        return (
            OMEGA * (real * inv_real - imag * inv_imag),
            OMEGA * (real * inv_imag + imag * inv_real),
        )

    def swapped(v):
        return jnp.concatenate([v[planes:], v[:planes]], axis=0)

    def shifts(v):
        zero = jnp.zeros((1, *size[1:]), F32)
        z_next = jnp.concatenate([v[1:planes], zero, v[planes + 1:], zero], axis=0)
        z_last = jnp.concatenate([zero, v[:planes - 1], zero, v[planes:-1]], axis=0)
        x_next = pltpu.roll(v, rows - 1, 1)
        x_next = jnp.where(row_at == rows - 1, swapped(x_next), x_next)
        x_last = pltpu.roll(v, 1, 1)
        x_last = jnp.where(row_at == 0, swapped(x_last), x_last)
        return z_next, z_last, x_next, x_last, pltpu.roll(v, size[2] - 1, 2), pltpu.roll(v, 1, 2)

    def helm(v, around):
        z_next, z_last, x_next, x_last, y_next, y_last = around
        return diag * v - (z_next + z_last + x_next + x_last + y_next + y_last)

    def update(real, imag):
        z_real, z_imag = precond(real, imag)
        image_real = helm(z_real, shifts(z_real)) - shift * z_imag
        image_imag = helm(z_imag, shifts(z_imag)) + shift * z_real
        more_real, more_imag = precond(real - image_real, imag - image_imag)
        return z_real + more_real, z_imag + more_imag

    source = right_part(0), right_part(1)
    first = [jnp.where(inside, v, 0.0) for v in update(*source)]
    slopes = [slope(f) for f in range(4)]
    residual = []
    for v, origin in zip(first, source):
        around = shifts(v)
        z_next, z_last, x_next, x_last, y_next, y_last = around
        surface = slopes[0] * v + slopes[1] * (z_next - z_last)
        surface = surface + slopes[2] * (x_next - x_last) + slopes[3] * (y_next - y_last)
        residual.append(jnp.where(inside, origin - helm(v, around) - surface, 0.0))
    for part in range(2):
        res_ref[part * planes:(part + 1) * planes] = residual[part][:planes, :, :cols]
    res_write = pltpu.make_async_copy(res_ref, res_hbm, written.at[0])
    res_write.start()
    second = update(*residual)
    for part in range(2):
        both = first[part] + second[part]
        sol_ref[part * planes:(part + 1) * planes] = both[:planes, :, :cols]
    sol_write = pltpu.make_async_copy(sol_ref, sol_hbm, written.at[1])
    sol_write.start()
    for there, _, copy in early_copies + late_copies:
        pl.when(there)(copy.wait_send)

    def finish_block(k, carry):
        block_copy(k).wait_send()
        return carry

    lax.fori_loop(1, n, finish_block, 0)
    res_write.wait()
    sol_write.wait()


def write_out(sol_ref, res_ref, sol_out, res_out, sol_held, res_held, here, done):
    loads = (
        pltpu.make_async_copy(sol_ref, sol_held, here.at[0]),
        pltpu.make_async_copy(res_ref, res_held, here.at[1]),
    )
    stores = (
        pltpu.make_async_copy(sol_held, sol_out, done.at[0]),
        pltpu.make_async_copy(res_held, res_out, done.at[1]),
    )
    for load in loads:
        load.start()
    for load, store in zip(loads, stores):
        load.wait()
        store.start()
    for store in stores:
        store.wait()


def per_device(
    n_gx, n_gy,
    rhs_field, permittivity, surf_dist, surf_normal, surf_inc, surf_cell, surf_mask, surf_owner,
):
    planes, rows, cols = permittivity.shape
    points = surf_cell.shape[1]
    n = n_gx * n_gy
    lines = planes * rows
    field = jax.ShapeDtypeStruct((2 * planes, rows, cols), F32)
    hbm = pl.BlockSpec(memory_space=pltpu.HBM)
    owner = surf_owner.reshape(1, -1)
    operands = (
        rhs_field.reshape(field.shape), permittivity, surf_dist, surf_normal, surf_inc,
        surf_cell, surf_mask, owner,
    )
    deep = GROUP * CAP * points
    sol, res = pl.pallas_call(
        functools.partial(kernel, n_gx, n_gy),
        out_shape=(field, field),
        in_specs=[hbm] * 8,
        out_specs=(hbm, hbm),
        scratch_shapes=[
            *[pltpu.VMEM(x.shape, x.dtype) for x in operands],
            pltpu.VMEM((n, ROWS, points), F32),
            pltpu.VMEM((n, ROWS, points), F32),
            pltpu.VMEM((PARTS * lines, deep), BF16),
            pltpu.VMEM((cols, deep), BF16),
            pltpu.VMEM((PARTS * lines, cols), F32),
            pltpu.VMEM((2 * planes, rows, cols), F32),
            pltpu.VMEM((2 * planes, rows, cols), F32),
            pltpu.VMEM((4 * planes, rows, cols), F32),
            pltpu.VMEM((4 * planes, rows, cols), F32),
            pltpu.VMEM((planes, rows, cols), F32),
            pltpu.VMEM((2, 4, 8, 2 * lines), F32),
            pltpu.VMEM((2, 3, 4, 8, 2 * lines), F32),
            pltpu.VMEM(field.shape, F32),
            pltpu.VMEM(field.shape, F32),
            pltpu.SemaphoreType.DMA((8,)),
            pltpu.SemaphoreType.DMA((2,)),
            pltpu.SemaphoreType.DMA((n,)),
            pltpu.SemaphoreType.DMA((n,)),
            pltpu.SemaphoreType.DMA((2, 10)),
            pltpu.SemaphoreType.DMA((2, 10)),
        ],
        compiler_params=pltpu.CompilerParams(
            collective_id=0, has_side_effects=True, vmem_limit_bytes=64 * 1024 * 1024
        ),
    )(*operands)
    sol, res = pl.pallas_call(
        write_out,
        out_shape=(field, field),
        in_specs=[hbm] * 2,
        out_specs=(hbm, hbm),
        scratch_shapes=[
            pltpu.VMEM(field.shape, F32),
            pltpu.VMEM(field.shape, F32),
            pltpu.SemaphoreType.DMA((2,)),
            pltpu.SemaphoreType.DMA((2,)),
        ],
        compiler_params=pltpu.CompilerParams(vmem_limit_bytes=64 * 1024 * 1024),
    )(sol, res)
    return sol.reshape(rhs_field.shape), res.reshape(rhs_field.shape)


def solution(mesh):
    placed = (
        P(None, None, "gx", "gy"),
        P(None, "gx", "gy"),
        P(("gx", "gy"), None),
        P(None, ("gx", "gy"), None),
        P(None, ("gx", "gy"), None),
        P(("gx", "gy"), None),
        P(("gx", "gy"), None),
        P(("gx", "gy"), None),
    )
    return jax.shard_map(
        functools.partial(per_device, mesh.shape["gx"], mesh.shape["gy"]),
        mesh=mesh,
        in_specs=placed,
        out_specs=(P(None, None, "gx", "gy"), P(None, None, "gx", "gy")),
        check_vma=False,
    )
```
